512 devices in a mesh: row: 8 (over y_hi, core), col: 64 (over z, y_lo, x).
Axes of the slice: x: 4, y: 8 (y_hi: 4, y_lo: 2; y = y_hi * 2 + y_lo), z: 8, core: 2. Of those that a mesh axis runs over, the one named last changes fastest.
Arguments:
- velocity: bfloat16 [3, 64, 1280, 1024], P(None, 'col', 'row'), may hold values from -6 to 6
- lengths: int32 [64, 8], P('col'), may hold values from 1 to 160, 1024 in all within a row
- inverse_x: float32 [4, 256, 256], replicated, as said below
- inverse_y: float32 [4, 256, 256], replicated, as said below
- metric: float32 [1024], replicated, may hold values from 0.25 to 4
Outputs:
- slope_x: bfloat16 [3, 64, 1024, 1024], P(None, None, 'col', 'row')
- slope_y: bfloat16 [3, 64, 1024, 1024], P(None, None, 'col', 'row')
The draws below stay inside these ranges and needn't reach their ends.
Inputs may be any that keep to these rules, and one draw needn't show every extreme that they name: For each plane, row index i uses its first lengths[z, i] slots; each plane's lengths sum to 1024 and their largest is 160. `inverse_x`: each block has a dominant diagonal. `inverse_y`: each block has a dominant diagonal.
All inputs are finite; a program needn't handle non-finite values.
Results may differ from the reference program's by a relative error of at most 0.001.
Values may be sent and summed in bfloat16 or wider, within the bound.
No kernel may reach another device: no remote copies, remote signals or barrier semaphores. Data moves between devices by JAX's collectives and lax.ppermute only.
A program may use at most 64 MiB of HBM per device.

```python
import math
import jax
import jax.numpy as jnp
import numpy as np
from jax import lax

NX = 1024
BS = 256
YCAP = 160
NY = 1024
NZ = 64
YROWS = 1280
N_ROW = 8


def dominant_blocks(key, blocks):
    first_key, second_key = jax.random.split(key)
    identity = jnp.eye(BS, dtype=jnp.float32)
    diagonal = jax.random.uniform(first_key, (blocks, BS, BS), jnp.float32, 0.7, 1.3)
    offdiag = jax.random.normal(second_key, (blocks, BS, BS), jnp.float32) * (0.5 / math.sqrt(BS))
    return identity * diagonal + (1.0 - identity) * offdiag


def draw_inverse_x(key, part):
    return dominant_blocks(jax.random.fold_in(key, 11), NX // BS)


def draw_inverse_y(key, part):
    return dominant_blocks(jax.random.fold_in(key, 23), NY // BS)


def block_scale(own_key, shape, pieces, low, high):
    def one(dim, blocks):
        steps = jax.random.uniform(jax.random.fold_in(jax.random.fold_in(own_key, 6), dim), (blocks,), jnp.float32, low / len(pieces), high / len(pieces))
        return jnp.repeat(jnp.exp(steps), shape[dim] // blocks).reshape((-1,) + (1,) * (len(shape) - dim - 1))

    loudness = one(*pieces[0])
    for cut in pieces[1:]:
        loudness = loudness * one(*cut)
    return loudness


def length_profile(amount, total, most, lean):
    loads = [(1 << 20) // math.isqrt(grade ** lean) + 1 for grade in range(2, amount + 1)]
    spare, holding = total - most - (amount - 1), [1] * (amount - 1)
    while spare > 0:
        candidates = [i for i in range(amount - 1) if holding[i] < most]
        mass, remaining = sum([loads[i] for i in candidates]), spare
        for i in candidates:
            extra = min(most - holding[i], max(1, remaining * loads[i] // mass), spare)
            holding[i] = holding[i] + extra
            spare = spare - extra
    return np.array([most] + holding)


def ragged_sizes(stream_key, amount, total, reach, slope):
    if amount == 2:
        one = jax.random.randint(stream_key, (), max(1, total - reach), min(reach, total - 1) + 1)
        return jnp.stack([one, total - one])
    tallies = jnp.asarray(length_profile(amount, total, reach, slope), jnp.int32)
    twos = (amount - 1) // 2
    source_of, sink = tallies[1:1 + 2 * twos:2], tallies[2:2 + 2 * twos:2]
    margin = jnp.minimum(source_of - 1, reach - sink)
    passed = jax.random.randint(jax.random.fold_in(stream_key, 1), (twos,), 0, 1 << 20) % (margin + 1)
    tallies = tallies.at[1:1 + 2 * twos:2].set(source_of - passed).at[2:2 + 2 * twos:2].set(sink + passed)
    return tallies[jax.random.permutation(jax.random.fold_in(stream_key, 2), amount)]


def centred(stream_key, dims, scale, bound, shards=(), held_as=jnp.bfloat16):
    entries = scale * jax.random.normal(stream_key, dims, jnp.float32)
    if shards:
        entries = entries * block_scale(stream_key, dims, shards, -0.22, 0.18)
    return jnp.clip(entries, -bound, bound).astype(held_as)


def setup_inputs(seed: int = 0) -> dict:
    arg_keys = jax.random.split(jax.random.key(seed), 6)
    velocity = centred(arg_keys[0], (3, NZ, YROWS, NX), 1.0, 6.0, ((1, 64), (2, 8)))
    lengths = jax.vmap(lambda own: ragged_sizes(own, N_ROW, NY, YCAP, 1))(jax.random.split(arg_keys[1], NZ)).reshape((NZ, N_ROW)).astype(jnp.int32)
    inverse_x = draw_inverse_x(jax.random.fold_in(arg_keys[5], 71), 0)
    inverse_y = draw_inverse_y(jax.random.fold_in(arg_keys[5], 71), 0)
    metric = jnp.clip(jnp.exp(jax.random.uniform(arg_keys[4], (NY,), jnp.float32, math.log(0.25), math.log(4.0))), 0.25, 4.0)
    return dict(velocity=velocity, lengths=lengths, inverse_x=inverse_x, inverse_y=inverse_y, metric=metric)


A_COEF = 14.0 / 9.0
B_COEF = 1.0 / 9.0
ALPHA = 1.0 / 3.0


def source_rows(lengths, grid_rows, capacity):
    row_ends = jnp.cumsum(lengths).astype(jnp.int32)
    starts = (row_ends - lengths).astype(jnp.int32)
    indices = jnp.arange(grid_rows, dtype=jnp.int32)
    owners = jnp.sum((indices[:, None] >= row_ends[None, :]).astype(jnp.int32), axis=1)
    ranks_all = jnp.arange(lengths.shape[0], dtype=jnp.int32)
    start_of = jnp.sum(jnp.where(ranks_all[None, :] == owners[:, None], starts[None, :], 0), axis=1)
    return (owners * capacity + indices - start_of).astype(jnp.int32)


def explicit_part(field, along):
    extent = field.shape[along]
    widths_pad = [(0, 0)] * field.ndim
    widths_pad[along] = (2, 2)
    padded = jnp.pad(field, widths_pad)

    def offset_slice(shift):
        return lax.slice_in_dim(padded, 2 + shift, 2 + shift + extent, axis=along)

    return (A_COEF / 2.0) * (offset_slice(1) - offset_slice(-1)) + (B_COEF / 4.0) * (offset_slice(2) - offset_slice(-2))


def apply_block(inverse, block_now, along):
    if along == 3:
        return jnp.einsum('cayj,ij->cayi', block_now, inverse, precision=lax.Precision.HIGHEST)
    return jnp.einsum('ij,cajx->caix', inverse, block_now, precision=lax.Precision.HIGHEST)


def block_solve(rhs, inverse, along):
    blocks = inverse.shape[0]
    width = inverse.shape[1]
    solved = []
    previous = None
    for number in range(blocks):
        block_now = lax.slice_in_dim(rhs, number * width, (number + 1) * width, axis=along)
        if previous is not None:
            head_row = lax.slice_in_dim(block_now, 0, 1, axis=along) - ALPHA * lax.slice_in_dim(previous, width - 1, width, axis=along)
            block_now = jnp.concatenate([head_row, lax.slice_in_dim(block_now, 1, width, axis=along)], axis=along)
        previous = apply_block(inverse[number], block_now, along)
        solved.append(previous)
    result = [None] * blocks
    result[blocks - 1] = solved[blocks - 1]
    for number in range(blocks - 2, -1, -1):
        shape_col = [1] * rhs.ndim
        shape_col[along] = width
        column = inverse[number][:, width - 1].reshape(shape_col)
        following = lax.slice_in_dim(result[number + 1], 0, 1, axis=along)
        result[number] = solved[number] - ALPHA * column * following
    return jnp.concatenate(result, axis=along)


def take_plane(values, sources):
    return jnp.take(values, sources, axis=1)


def reference(velocity, lengths, inverse_x, inverse_y, metric):
    grid_rows = metric.shape[0]
    sources = jax.vmap(lambda single: source_rows(single, grid_rows, YCAP))(lengths)
    packed = jax.vmap(take_plane, in_axes=(1, 0), out_axes=1)(velocity, sources)

    def component(field):
        values = field.astype(jnp.float32)
        along_x = block_solve(explicit_part(values, 3), inverse_x, 3).astype(jnp.bfloat16)
        along_y = (metric[:, None] * block_solve(explicit_part(values, 2), inverse_y, 2)).astype(jnp.bfloat16)
        return along_x, along_y

    result_x, result_y = lax.map(component, packed[:, None])
    return result_x[:, 0], result_y[:, 0]
```

```python
import jax
import jax.numpy as jnp
from jax import lax
from jax.experimental import pallas as pl
from jax.experimental.pallas import tpu as pltpu
from jax.sharding import PartitionSpec as P

A2 = 14.0 / 9.0 / 2.0
B4 = 1.0 / 9.0 / 4.0
ALPHA = 1.0 / 3.0
F32 = jnp.float32
BF16 = jnp.bfloat16
NT = (((1,), (1,)), ((), ()))
MIB = 1 << 20


def lanes(shape):
    return lax.broadcasted_iota(jnp.int32, shape, len(shape) - 1)


def sublanes(shape):
    return lax.broadcasted_iota(jnp.int32, shape, len(shape) - 2)


def split(value):
    high = value.astype(BF16)
    return high, (value - high.astype(F32)).astype(BF16)


def roll(value, shift):
    return pltpu.roll(value, shift % value.shape[-1], value.ndim - 1)


def stencil(rows):
    return A2 * (roll(rows, 1) - roll(rows, -1)) + B4 * (roll(rows, 2) - roll(rows, -2))


def stencil_line(rows):
    width = rows.shape[-1]
    lane = lanes(rows.shape)

    def shifted(by):
        inside = lane >= by if by > 0 else lane < width + by
        return jnp.where(inside, roll(rows, by), 0.0)

    return A2 * (shifted(1) - shifted(-1)) + B4 * (shifted(2) - shifted(-2))


def coupling_rows(first, last, blocks, width):
    total = blocks * width

    def place(row, k):
        parts = []
        if k:
            parts.append(jnp.zeros((1, k * width), F32))
        parts.append(row)
        if k < blocks - 1:
            parts.append(jnp.zeros((1, (blocks - 1 - k) * width), F32))
        return jnp.concatenate(parts, axis=1)

    stacked = jnp.concatenate(
        [place(last[k], k) for k in range(blocks)] + [place(first[k], k) for k in range(blocks)], axis=0
    )
    applied = stencil_line(stacked)
    g_last = []
    for k in range(blocks):
        row = applied[k : k + 1]
        if k:
            row = row - ALPHA * last[k][:, 0:1] * g_last[k - 1]
        g_last.append(row)
    u_first = [None] * blocks
    for k in range(blocks - 1, -1, -1):
        row = applied[blocks + k : blocks + k + 1]
        if k:
            row = row - ALPHA * first[k][:, 0:1] * g_last[k - 1]
        if k < blocks - 1:
            row = row - ALPHA * first[k][:, width - 1 : width] * u_first[k + 1]
        u_first[k] = row
    return g_last, u_first


def pack_kernel(vel, inv, out, heads, tails, sems):
    blocks, width = inv.shape[0], inv.shape[1]
    line = blocks * width
    copy_heads = pltpu.make_async_copy(inv.at[:, pl.ds(0, 16), :], heads, sems.at[0])
    copy_tails = pltpu.make_async_copy(inv.at[:, pl.ds(width - 16, 16), :], tails, sems.at[1])
    copy_heads.start()
    copy_tails.start()
    comps = vel.shape[0]
    for i in range(out.shape[0]):
        columns = slice(128 * i, 128 * i + 128)
        for c in range(comps):
            out[i, 128 * c : 128 * c + 128, :] = vel[c, 0:128, columns]
            out[i, 384 + 32 * c : 416 + 32 * c, :] = vel[c, 128:160, columns]
    copy_heads.wait()
    copy_tails.wait()
    first = [heads[k, 0:1, :] for k in range(blocks)]
    last = [tails[k, 15:16, :] for k in range(blocks)]
    g_last, u_first = coupling_rows(first, last, blocks, width)
    lane = lanes((1, line))
    zero = jnp.zeros((1, line), F32)

    def unit(at):
        return jnp.where(lane == at, 1.0, 0.0)

    rows = []
    for k in range(blocks):
        lo, hi = width * k, width * (k + 1)
        before, after, tip, end = zero, zero, zero, zero
        if k:
            before = -A2 * unit(lo - 1) - B4 * unit(lo - 2) - ALPHA * g_last[k - 1]
            tip = unit(lo - 1)
        if k < blocks - 1:
            after = A2 * unit(hi) + B4 * unit(hi + 1) - ALPHA * u_first[k + 1]
            end = unit(hi)
        rows += [before, before, tip, end, after, after, zero, zero]
    weights = jnp.concatenate(rows, axis=0)
    high, low = split(weights)
    both = jnp.concatenate([high, low], axis=0)
    pieces = [vel[c, 0:128, :] for c in range(comps)]
    pieces += [vel[c, 128:160, :] for c in range(comps)] + [jnp.zeros((32, line), BF16)]
    count = 8 * blocks
    coded = []
    for piece in (pieces[0], pieces[1], pieces[2], jnp.concatenate(pieces[3:], axis=0)):
        value = lax.dot_general(both, piece, NT, preferred_element_type=F32)
        value = value[0:count] + value[count : 2 * count]
        top = value.astype(BF16).astype(F32)
        place = sublanes(value.shape) % 8
        coded.append(jnp.where((place == 1) | (place == 5), value - top, top))
    for k in range(blocks):
        block = jnp.concatenate([part[8 * k : 8 * k + 8] for part in coded], axis=0).astype(BF16)
        out[2 * k, 480:512, :] = block
        out[2 * k + 1, 480:512, :] = block


def pack(velocity, inverse_x):
    comps, slots, line = velocity.shape
    blocks, width, _ = inverse_x.shape
    return pl.pallas_call(
        pack_kernel,
        out_shape=jax.ShapeDtypeStruct((line // 128, 512, 128), BF16),
        in_specs=[pl.BlockSpec(memory_space=pltpu.VMEM), pl.BlockSpec(memory_space=pl.ANY)],
        out_specs=pl.BlockSpec(memory_space=pltpu.VMEM),
        scratch_shapes=[
            pltpu.VMEM((blocks, 16, width), F32),
            pltpu.VMEM((blocks, 16, width), F32),
            pltpu.SemaphoreType.DMA((2,)),
        ],
        compiler_params=pltpu.CompilerParams(vmem_limit_bytes=24 * MIB),
    )(velocity, inverse_x)


def weights_kernel(where, inv_x, inv_y, metric, out_y, out_x, own, sem):
    blocks, width = inv_y.shape[0], inv_y.shape[1]
    copy = pltpu.make_async_copy(inv_x.at[where[0], pl.ds(where[1] * 128, 128), :], own, sem)
    copy.start()
    first = [inv_y[k, 0:1, :] for k in range(blocks)]
    last = [inv_y[k, width - 1 : width, :] for k in range(blocks)]
    g_last, u_first = coupling_rows(first, last, blocks, width)
    size = blocks * width
    for k in range(blocks):
        for half in range(width // 128):
            here = slice(128 * half, 128 * half + 128)
            tile = inv_y[k, here, :]
            side = jnp.zeros((128, 128), F32)
            local = stencil(jnp.concatenate([side, tile, side], axis=1))
            parts = []
            if k > 1:
                parts.append(jnp.zeros((128, (k - 1) * width + 128), F32))
            elif k:
                parts.append(jnp.zeros((128, 128), F32))
            begin = 0 if k else 128
            end = 512 if k < blocks - 1 else 384
            parts.append(local[:, begin:end])
            rest = size - (k * width + (end - 128))
            if rest:
                parts.append(jnp.zeros((128, rest), F32))
            full = jnp.concatenate(parts, axis=1) if len(parts) > 1 else parts[0]
            if k:
                full = full - tile[:, 0:1] * (ALPHA * g_last[k - 1])
            if k < blocks - 1:
                full = full - tile[:, width - 1 : width] * (ALPHA * u_first[k + 1])
            at = k * width + 128 * half
            scale = jnp.broadcast_to(metric[at // 128 : at // 128 + 1, :], (128, 128)).T
            full = full * jnp.concatenate([scale] * (size // 128), axis=1)
            high, low = split(full)
            out_y[0, at : at + 128, :] = high
            out_y[1, at : at + 128, :] = low
    copy.wait()
    tile = own[...]
    side = jnp.zeros((128, 128), F32)
    local = stencil(jnp.concatenate([side, tile, side], axis=1))
    left, right = local[:, 128:256], local[:, 256:384]
    flip = where[1] == 0
    mine = jnp.where(flip, left, right)
    other = jnp.where(flip, right, left)
    lane = lanes((128, 128))
    parts = [mine, other]
    for c in range(3):
        at = lane - 8 * c
        value = jnp.where((at == 0) | (at == 1), tile[:, 0:1], 0.0)
        value = jnp.where(at == 2, -B4 * tile[:, 1:2], value)
        value = jnp.where(at == 3, B4 * tile[:, width - 2 : width - 1], value)
        value = jnp.where((at == 4) | (at == 5), tile[:, width - 1 : width], value)
        parts.append(value)
    high, low = split(jnp.concatenate(parts, axis=1))
    out_x[0:128, :] = high
    out_x[128:256, :] = low


def build_weights(where, inverse_x, inverse_y, metric):
    blocks, width, _ = inverse_y.shape
    size = blocks * width
    return pl.pallas_call(
        weights_kernel,
        out_shape=(
            jax.ShapeDtypeStruct((2, size, size), BF16),
            jax.ShapeDtypeStruct((256, 640), BF16),
        ),
        in_specs=[
            pl.BlockSpec(memory_space=pltpu.SMEM),
            pl.BlockSpec(memory_space=pl.ANY),
            pl.BlockSpec(memory_space=pltpu.VMEM),
            pl.BlockSpec(memory_space=pltpu.VMEM),
        ],
        out_specs=(pl.BlockSpec(memory_space=pltpu.VMEM), pl.BlockSpec(memory_space=pltpu.VMEM)),
        scratch_shapes=[pltpu.VMEM((128, width), F32), pltpu.SemaphoreType.DMA],
        compiler_params=pltpu.CompilerParams(vmem_limit_bytes=32 * MIB),
        cost_estimate=pl.CostEstimate(flops=20_000_000, bytes_accessed=6_000_000, transcendentals=0),
    )(where, inverse_x, inverse_y, metric)


def compact_kernel(lengths, recv, packed, extras):
    sources = recv.shape[0]
    starts, total = [], jnp.int32(0)
    for s in range(sources):
        starts.append(total)
        total = total + lengths[0, s]
    targets = []
    lane = lanes((1, 256))
    for tile in range(5):
        if tile < 4:
            slot = lane % 128
            source = lane // 128 + 2 * tile
            names = (2 * tile, 2 * tile + 1)
        else:
            slot = 128 + lane % 32
            source = lane // 32
            names = range(sources)
        target = jnp.full((1, 256), -1, jnp.int32)
        for s in names:
            target = jnp.where((source == s) & (slot < lengths[0, s]), starts[s] + slot, target)
        targets.append(target)
    coded = [recv[s, 480:512, :].astype(F32) for s in range(sources)]
    pad = jnp.zeros((104, 256), F32)
    small = lanes((8, 128)) // 32
    data, feats = [], []
    for tile in range(5):
        columns = []
        for c in range(3):
            if tile < 4:
                block = recv[2 * tile : 2 * tile + 2, 128 * c : 128 * c + 128, :]
            else:
                block = recv[:, 384 + 32 * c : 416 + 32 * c, :]
            columns.append(block.reshape(256, 128))
        data.append(jnp.concatenate(columns, axis=1))
        if tile < 4:
            block = jnp.concatenate([coded[2 * tile][0:24], coded[2 * tile + 1][0:24]], axis=1)
        else:
            halves = []
            for first in (0, 4):
                rows = []
                for c in range(3):
                    value = jnp.zeros((8, 128), F32)
                    for q in range(4):
                        value = jnp.where(small == q, roll(coded[first + q][24:32], 32 * (q - c)), value)
                    rows.append(value)
                halves.append(jnp.concatenate(rows, axis=0))
            block = jnp.concatenate(halves, axis=1)
        feats.append(jnp.concatenate([block, pad], axis=0).astype(BF16))
    for part in range(4):
        row = sublanes((256, 256)) + 256 * part
        sums = jnp.zeros((256, 384), F32)
        coupled = jnp.zeros((256, 128), F32)
        for tile in range(5):
            pick = jnp.where(row == targets[tile], 1.0, 0.0).astype(BF16)
            sums = sums + jnp.dot(pick, data[tile], preferred_element_type=F32)
            coupled = coupled + lax.dot_general(pick, feats[tile], NT, preferred_element_type=F32)
        packed[256 * part : 256 * part + 256, :] = sums.astype(BF16)
        extras[256 * part : 256 * part + 256, :] = coupled.astype(BF16)


def compact(lengths, recv):
    return pl.pallas_call(
        compact_kernel,
        out_shape=(jax.ShapeDtypeStruct((1024, 384), BF16), jax.ShapeDtypeStruct((1024, 128), BF16)),
        in_specs=[pl.BlockSpec(memory_space=pltpu.SMEM), pl.BlockSpec(memory_space=pltpu.VMEM)],
        out_specs=(pl.BlockSpec(memory_space=pltpu.VMEM), pl.BlockSpec(memory_space=pltpu.VMEM)),
        compiler_params=pltpu.CompilerParams(vmem_limit_bytes=24 * MIB),
    )(lengths, recv)


def normal_kernel(packed, weights, out, held, sem):
    field = packed[...]
    for part in range(4):
        here = slice(256 * part, 256 * part + 256)
        value = jnp.dot(weights[0, here, :], field, preferred_element_type=F32)
        value = value + jnp.dot(weights[1, here, :], field, preferred_element_type=F32)
        for c in range(3):
            held[16 * part : 16 * part + 16, 16 * c : 16 * c + 16, :] = (
                value[:, 128 * c : 128 * c + 128].astype(BF16).reshape(16, 16, 128)
            )
    copy = pltpu.make_async_copy(held, out.at[:, pl.ds(48, 48), :], sem)
    copy.start()
    copy.wait()


def normal(packed, weights):
    return pl.pallas_call(
        normal_kernel,
        out_shape=jax.ShapeDtypeStruct((64, 96, 128), BF16),
        in_specs=[pl.BlockSpec(memory_space=pltpu.VMEM), pl.BlockSpec(memory_space=pltpu.VMEM)],
        out_specs=pl.BlockSpec(memory_space=pl.ANY),
        scratch_shapes=[pltpu.VMEM((64, 48, 128), BF16), pltpu.SemaphoreType.DMA],
        compiler_params=pltpu.CompilerParams(vmem_limit_bytes=24 * MIB),
        cost_estimate=pl.CostEstimate(flops=1_600_000_000, bytes_accessed=6_000_000, transcendentals=0),
    )(packed, weights)


def stream_kernel(packed, partner, extras, weights, sent, out, held, sem):
    del sent
    coupled = extras[...]
    for c in range(3):
        columns = slice(128 * c, 128 * c + 128)
        field = jnp.concatenate([packed[:, columns], partner[:, columns]], axis=1)
        value = lax.dot_general(field, weights[:, 0:256], NT, preferred_element_type=F32)
        value = value + lax.dot_general(
            coupled, weights[:, 256 + 128 * c : 384 + 128 * c], NT, preferred_element_type=F32
        )
        value = value[:, 0:128] + value[:, 128:256]
        held[:, 16 * c : 16 * c + 16, :] = value.astype(BF16).reshape(64, 16, 128)
    copy = pltpu.make_async_copy(held, out.at[:, pl.ds(0, 48), :], sem)
    copy.start()
    copy.wait()


def stream(packed, partner, extras, weights, sent):
    vmem = pl.BlockSpec(memory_space=pltpu.VMEM)
    return pl.pallas_call(
        stream_kernel,
        out_shape=jax.ShapeDtypeStruct((64, 96, 128), BF16),
        in_specs=[vmem, vmem, vmem, vmem, pl.BlockSpec(memory_space=pl.ANY)],
        out_specs=pl.BlockSpec(memory_space=pl.ANY),
        scratch_shapes=[pltpu.VMEM((64, 48, 128), BF16), pltpu.SemaphoreType.DMA],
        input_output_aliases={4: 0},
        compiler_params=pltpu.CompilerParams(vmem_limit_bytes=24 * MIB),
    )(packed, partner, extras, weights, sent)


def unpack_kernel(recv, out_x, out_y, sems):
    copies = []
    for which, out in enumerate((out_x, out_y)):
        for c in range(3):
            copies.append(
                pltpu.make_async_copy(
                    recv.at[:, pl.ds(48 * which + 16 * c, 16), :], out.at[c], sems.at[3 * which + c]
                )
            )
    for copy in copies:
        copy.start()
    for copy in copies:
        copy.wait()


def unpack(recv):
    shape = jax.ShapeDtypeStruct((3, 64, 16, 128), BF16)
    anywhere = pl.BlockSpec(memory_space=pl.ANY)
    return pl.pallas_call(
        unpack_kernel,
        out_shape=(shape, shape),
        in_specs=[anywhere],
        out_specs=(anywhere, anywhere),
        scratch_shapes=[pltpu.SemaphoreType.DMA((6,))],
        compiler_params=pltpu.CompilerParams(vmem_limit_bytes=16 * MIB),
    )(recv)


def local(velocity, lengths, inverse_x, inverse_y, metric):
    rank = lax.axis_index("row")
    where = jnp.stack([rank // 2, rank % 2]).astype(jnp.int32)
    sent = pack(velocity[:, 0], inverse_x)
    weights_y, weights_x = build_weights(where, inverse_x, inverse_y, metric.reshape(8, 128))
    received = lax.all_to_all(sent, "row", split_axis=0, concat_axis=0, tiled=True)
    packed, extras = compact(lengths, received)
    partner = lax.ppermute(packed, "row", [(i, i ^ 1) for i in range(8)])
    result = normal(packed, weights_y)
    result = stream(packed, partner, extras, weights_x, result)
    moved = lax.all_to_all(result, "col", split_axis=0, concat_axis=0, tiled=True)
    return unpack(moved)


def solution(mesh):
    return jax.shard_map(
        local,
        mesh=mesh,
        in_specs=(P(None, "col", "row", None), P("col", None), P(), P(), P()),
        out_specs=(P(None, None, "col", "row"), P(None, None, "col", "row")),
        check_vma=False,
    )
```

```python
import jax
import jax.numpy as jnp
from jax import lax
from jax.experimental import pallas as pl
from jax.experimental.pallas import tpu as pltpu
from jax.sharding import PartitionSpec as P

A2 = 14.0 / 9.0 / 2.0
B4 = 1.0 / 9.0 / 4.0
ALPHA = 1.0 / 3.0
F32 = jnp.float32
BF16 = jnp.bfloat16
NT = (((1,), (1,)), ((), ()))
MIB = 1 << 20
fixed = pltpu.with_memory_space_constraint
ROW = (4, 5, 0, 1, 6, 7, 2, 3)
COL = (7, 6, 5, 4, 3, 2, 1, 0)
SPANS = ((0, 48), (48, 48), (96, 64))


def lanes(shape):
    return lax.broadcasted_iota(jnp.int32, shape, len(shape) - 1)


def sublanes(shape):
    return lax.broadcasted_iota(jnp.int32, shape, len(shape) - 2)


def split(value):
    high = value.astype(BF16)
    return high, (value - high.astype(F32)).astype(BF16)


def roll(value, shift):
    return pltpu.roll(value, shift % value.shape[-1], value.ndim - 1)


def stencil(rows):
    return A2 * (roll(rows, 1) - roll(rows, -1)) + B4 * (roll(rows, 2) - roll(rows, -2))


def stencil_line(rows):
    width = rows.shape[-1]
    lane = lanes(rows.shape)

    def shifted(by):
        inside = lane >= by if by > 0 else lane < width + by
        return jnp.where(inside, roll(rows, by), 0.0)

    return A2 * (shifted(1) - shifted(-1)) + B4 * (shifted(2) - shifted(-2))


def coupling_rows(first, last, blocks, width):
    total = blocks * width

    def place(row, k):
        parts = []
        if k:
            parts.append(jnp.zeros((1, k * width), F32))
        parts.append(row)
        if k < blocks - 1:
            parts.append(jnp.zeros((1, (blocks - 1 - k) * width), F32))
        return jnp.concatenate(parts, axis=1)

    stacked = jnp.concatenate(
        [place(last[k], k) for k in range(blocks)] + [place(first[k], k) for k in range(blocks)], axis=0
    )
    applied = stencil_line(stacked)
    g_last = []
    for k in range(blocks):
        row = applied[k : k + 1]
        if k:
            row = row - ALPHA * last[k][:, 0:1] * g_last[k - 1]
        g_last.append(row)
    u_first = [None] * blocks
    for k in range(blocks - 1, -1, -1):
        row = applied[blocks + k : blocks + k + 1]
        if k:
            row = row - ALPHA * first[k][:, 0:1] * g_last[k - 1]
        if k < blocks - 1:
            row = row - ALPHA * first[k][:, width - 1 : width] * u_first[k + 1]
        u_first[k] = row
    return g_last, u_first


def pack_kernel(vel_hbm, inv, out, vel, heads, tails, sems):
    blocks, width = inv.shape[0], inv.shape[1]
    line = blocks * width
    copy_heads = pltpu.make_async_copy(inv.at[:, pl.ds(0, 16), :], heads, sems.at[0])
    copy_tails = pltpu.make_async_copy(inv.at[:, pl.ds(width - 16, 16), :], tails, sems.at[1])
    copy_heads.start()
    copy_tails.start()
    comps = vel.shape[0]
    copies = []
    for c in range(comps):
        for number, (begin, size) in enumerate(SPANS):
            here = (c, pl.ds(begin, size))
            copy = pltpu.make_async_copy(vel_hbm.at[here], vel.at[here], sems.at[2 + len(SPANS) * c + number])
            copy.start()
            copies.append(copy)
    copy_heads.wait()
    copy_tails.wait()
    first = [heads[k, 0:1, :] for k in range(blocks)]
    last = [tails[k, 15:16, :] for k in range(blocks)]
    g_last, u_first = coupling_rows(first, last, blocks, width)
    lane = lanes((1, line))
    zero = jnp.zeros((1, line), F32)

    def unit(at):
        return jnp.where(lane == at, 1.0, 0.0)

    rows = []
    for k in range(blocks):
        lo, hi = width * k, width * (k + 1)
        before, after, tip, end = zero, zero, zero, zero
        if k:
            before = -A2 * unit(lo - 1) - B4 * unit(lo - 2) - ALPHA * g_last[k - 1]
            tip = unit(lo - 1)
        if k < blocks - 1:
            after = A2 * unit(hi) + B4 * unit(hi + 1) - ALPHA * u_first[k + 1]
            end = unit(hi)
        rows += [before, before, tip, end, after, after, zero, zero]
    weights = jnp.concatenate(rows, axis=0)
    high, low = split(weights)
    both = jnp.concatenate([high, low], axis=0)
    for copy in copies:
        copy.wait()
    for i in range(out.shape[0]):
        columns = slice(128 * ROW[i], 128 * ROW[i] + 128)
        for c in range(comps):
            out[i, 128 * c : 128 * c + 128, :] = vel[c, 0:128, columns]
            out[i, 384 + 32 * c : 416 + 32 * c, :] = vel[c, 128:160, columns]
    pieces = [vel[c, 0:128, :] for c in range(comps)]
    pieces += [vel[c, 128:160, :] for c in range(comps)] + [jnp.zeros((32, line), BF16)]
    count = 8 * blocks
    coded = []
    for piece in (pieces[0], pieces[1], pieces[2], jnp.concatenate(pieces[3:], axis=0)):
        value = lax.dot_general(both, piece, NT, preferred_element_type=F32)
        value = value[0:count] + value[count : 2 * count]
        top = value.astype(BF16).astype(F32)
        place = sublanes(value.shape) % 8
        coded.append(jnp.where((place == 1) | (place == 5), value - top, top))
    for k in range(blocks):
        block = jnp.concatenate([part[8 * k : 8 * k + 8] for part in coded], axis=0).astype(BF16)
        out[ROW.index(2 * k), 480:512, :] = block
        out[ROW.index(2 * k + 1), 480:512, :] = block


def pack(velocity, inverse_x):
    comps, slots, line = velocity.shape
    blocks, width, _ = inverse_x.shape
    return pl.pallas_call(
        pack_kernel,
        out_shape=jax.ShapeDtypeStruct((line // 128, 512, 128), BF16),
        in_specs=[pl.BlockSpec(memory_space=pltpu.HBM), pl.BlockSpec(memory_space=pltpu.HBM)],
        out_specs=pl.BlockSpec(memory_space=pltpu.VMEM),
        scratch_shapes=[
            pltpu.VMEM(velocity.shape, BF16),
            pltpu.VMEM((blocks, 16, width), F32),
            pltpu.VMEM((blocks, 16, width), F32),
            pltpu.SemaphoreType.DMA((2 + len(SPANS) * comps,)),
        ],
        compiler_params=pltpu.CompilerParams(vmem_limit_bytes=24 * MIB),
    )(fixed(velocity, pltpu.HBM), fixed(inverse_x, pltpu.HBM))


def weights_kernel(where, inv_x, inv_y, metric, out_y, out_x, own, sem):
    blocks, width = inv_y.shape[0], inv_y.shape[1]
    copy = pltpu.make_async_copy(inv_x.at[where[0], pl.ds(where[1] * 128, 128), :], own, sem)
    copy.start()
    first = [inv_y[k, 0:1, :] for k in range(blocks)]
    last = [inv_y[k, width - 1 : width, :] for k in range(blocks)]
    g_last, u_first = coupling_rows(first, last, blocks, width)
    size = blocks * width
    for k in range(blocks):
        for half in range(width // 128):
            here = slice(128 * half, 128 * half + 128)
            tile = inv_y[k, here, :]
            side = jnp.zeros((128, 128), F32)
            local = stencil(jnp.concatenate([side, tile, side], axis=1))
            parts = []
            if k > 1:
                parts.append(jnp.zeros((128, (k - 1) * width + 128), F32))
            elif k:
                parts.append(jnp.zeros((128, 128), F32))
            begin = 0 if k else 128
            end = 512 if k < blocks - 1 else 384
            parts.append(local[:, begin:end])
            rest = size - (k * width + (end - 128))
            if rest:
                parts.append(jnp.zeros((128, rest), F32))
            full = jnp.concatenate(parts, axis=1) if len(parts) > 1 else parts[0]
            if k:
                full = full - tile[:, 0:1] * (ALPHA * g_last[k - 1])
            if k < blocks - 1:
                full = full - tile[:, width - 1 : width] * (ALPHA * u_first[k + 1])
            at = k * width + 128 * half
            scale = jnp.broadcast_to(metric[at // 128 : at // 128 + 1, :], (128, 128)).T
            full = full * jnp.concatenate([scale] * (size // 128), axis=1)
            high, low = split(full)
            out_y[0, at : at + 128, :] = high
            out_y[1, at : at + 128, :] = low
    copy.wait()
    tile = own[...]
    side = jnp.zeros((128, 128), F32)
    local = stencil(jnp.concatenate([side, tile, side], axis=1))
    left, right = local[:, 128:256], local[:, 256:384]
    flip = where[1] == 0
    mine = jnp.where(flip, left, right)
    other = jnp.where(flip, right, left)
    lane = lanes((128, 128))
    parts = [mine, other]
    for c in range(3):
        at = lane - 8 * c
        value = jnp.where((at == 0) | (at == 1), tile[:, 0:1], 0.0)
        value = jnp.where(at == 2, -B4 * tile[:, 1:2], value)
        value = jnp.where(at == 3, B4 * tile[:, width - 2 : width - 1], value)
        value = jnp.where((at == 4) | (at == 5), tile[:, width - 1 : width], value)
        parts.append(value)
    high, low = split(jnp.concatenate(parts, axis=1))
    out_x[0:128, :] = high
    out_x[128:256, :] = low


def build_weights(where, inverse_x, inverse_y, metric):
    blocks, width, _ = inverse_y.shape
    size = blocks * width
    return pl.pallas_call(
        weights_kernel,
        out_shape=(
            jax.ShapeDtypeStruct((2, size, size), BF16),
            jax.ShapeDtypeStruct((256, 640), BF16),
        ),
        in_specs=[
            pl.BlockSpec(memory_space=pltpu.SMEM),
            pl.BlockSpec(memory_space=pl.ANY),
            pl.BlockSpec(memory_space=pltpu.VMEM),
            pl.BlockSpec(memory_space=pltpu.VMEM),
        ],
        out_specs=(pl.BlockSpec(memory_space=pltpu.VMEM), pl.BlockSpec(memory_space=pltpu.VMEM)),
        scratch_shapes=[pltpu.VMEM((128, width), F32), pltpu.SemaphoreType.DMA],
        compiler_params=pltpu.CompilerParams(vmem_limit_bytes=32 * MIB),
        cost_estimate=pl.CostEstimate(flops=20_000_000, bytes_accessed=6_000_000, transcendentals=0),
    )(where, inverse_x, inverse_y, metric)


def compact_kernel(lengths, recv, packed, extras):
    sources = recv.shape[0]
    starts, total = [], jnp.int32(0)
    for s in range(sources):
        starts.append(total)
        total = total + lengths[0, s]
    targets = []
    lane = lanes((1, 256))
    for tile in range(5):
        if tile < 4:
            slot = lane % 128
            source = lane // 128 + 2 * tile
            names = (2 * tile, 2 * tile + 1)
        else:
            slot = 128 + lane % 32
            source = lane // 32
            names = range(sources)
        target = jnp.full((1, 256), -1, jnp.int32)
        for s in names:
            held = (source == s) & (slot < lengths[0, ROW[s]])
            target = jnp.where(held, starts[ROW[s]] + slot, target)
        targets.append(target)
    coded = [recv[s, 480:512, :].astype(F32) for s in range(sources)]
    pad = jnp.zeros((104, 256), F32)
    small = lanes((8, 128)) // 32
    data, feats = [], []
    for tile in range(5):
        columns = []
        for c in range(3):
            if tile < 4:
                block = recv[2 * tile : 2 * tile + 2, 128 * c : 128 * c + 128, :]
            else:
                block = recv[:, 384 + 32 * c : 416 + 32 * c, :]
            columns.append(block.reshape(256, 128))
        data.append(jnp.concatenate(columns, axis=1))
        if tile < 4:
            block = jnp.concatenate([coded[2 * tile][0:24], coded[2 * tile + 1][0:24]], axis=1)
        else:
            halves = []
            for first in (0, 4):
                rows = []
                for c in range(3):
                    value = jnp.zeros((8, 128), F32)
                    for q in range(4):
                        value = jnp.where(small == q, roll(coded[first + q][24:32], 32 * (q - c)), value)
                    rows.append(value)
                halves.append(jnp.concatenate(rows, axis=0))
            block = jnp.concatenate(halves, axis=1)
        feats.append(jnp.concatenate([block, pad], axis=0).astype(BF16))
    for part in range(4):
        row = sublanes((256, 256)) + 256 * part
        sums = jnp.zeros((256, 384), F32)
        coupled = jnp.zeros((256, 128), F32)
        for tile in range(5):
            pick = jnp.where(row == targets[tile], 1.0, 0.0).astype(BF16)
            sums = sums + jnp.dot(pick, data[tile], preferred_element_type=F32)
            coupled = coupled + lax.dot_general(pick, feats[tile], NT, preferred_element_type=F32)
        packed[256 * part : 256 * part + 256, :] = sums.astype(BF16)
        extras[256 * part : 256 * part + 256, :] = coupled.astype(BF16)


def compact(lengths, recv):
    return pl.pallas_call(
        compact_kernel,
        out_shape=(jax.ShapeDtypeStruct((1024, 384), BF16), jax.ShapeDtypeStruct((1024, 128), BF16)),
        in_specs=[pl.BlockSpec(memory_space=pltpu.SMEM), pl.BlockSpec(memory_space=pltpu.VMEM)],
        out_specs=(pl.BlockSpec(memory_space=pltpu.VMEM), pl.BlockSpec(memory_space=pltpu.VMEM)),
        compiler_params=pltpu.CompilerParams(vmem_limit_bytes=24 * MIB),
    )(lengths, recv)


def normal_kernel(packed, weights_hbm, out, held, weights, sems, loads):
    field = packed[...]
    copies, fetches = [], []
    for part in range(4):
        here = (slice(None), pl.ds(256 * part, 256))
        fetches.append(pltpu.make_async_copy(weights_hbm.at[here], weights.at[here], loads.at[part]))
        fetches[-1].start()
    for part in range(4):
        here = slice(256 * part, 256 * part + 256)
        fetches[part].wait()
        value = jnp.dot(weights[0, here, :], field, preferred_element_type=F32)
        value = value + jnp.dot(weights[1, here, :], field, preferred_element_type=F32)
        for c in range(3):
            block = value[:, 128 * c : 128 * c + 128].astype(BF16).reshape(16, 16, 128)
            for half in range(2):
                at = 8 * COL.index(2 * part + half)
                held[at : at + 8, 16 * c : 16 * c + 16, :] = block[8 * half : 8 * half + 8]
        for half in range(2):
            rows = pl.ds(8 * COL.index(2 * part + half), 8)
            copy = pltpu.make_async_copy(
                held.at[rows], out.at[rows, pl.ds(48, 48), :], sems.at[2 * part + half]
            )
            copy.start()
            copies.append(copy)
    for copy in copies:
        copy.wait()


def normal(packed, weights):
    return pl.pallas_call(
        normal_kernel,
        out_shape=jax.ShapeDtypeStruct((64, 96, 128), BF16),
        in_specs=[pl.BlockSpec(memory_space=pltpu.VMEM), pl.BlockSpec(memory_space=pltpu.HBM)],
        out_specs=pl.BlockSpec(memory_space=pl.ANY),
        scratch_shapes=[
            pltpu.VMEM((64, 48, 128), BF16),
            pltpu.VMEM(weights.shape, BF16),
            pltpu.SemaphoreType.DMA((8,)),
            pltpu.SemaphoreType.DMA((4,)),
        ],
        compiler_params=pltpu.CompilerParams(vmem_limit_bytes=24 * MIB),
        cost_estimate=pl.CostEstimate(flops=1_600_000_000, bytes_accessed=6_000_000, transcendentals=0),
    )(packed, fixed(weights, pltpu.HBM))


def stream_kernel(packed, partner, extras, weights, sent, out, held, sems):
    del sent
    copies = []
    coupled = extras[...]
    for c in range(3):
        columns = slice(128 * c, 128 * c + 128)
        field = jnp.concatenate([packed[:, columns], partner[:, columns]], axis=1)
        value = lax.dot_general(field, weights[:, 0:256], NT, preferred_element_type=F32)
        value = value + lax.dot_general(
            coupled, weights[:, 256 + 128 * c : 384 + 128 * c], NT, preferred_element_type=F32
        )
        value = value[:, 0:128] + value[:, 128:256]
        rows = pl.ds(16 * c, 16)
        block = value.astype(BF16).reshape(64, 16, 128)
        for run in range(8):
            at = 8 * COL.index(run)
            held[at : at + 8, 16 * c : 16 * c + 16, :] = block[8 * run : 8 * run + 8]
        copy = pltpu.make_async_copy(held.at[:, rows, :], out.at[:, rows, :], sems.at[c])
        copy.start()
        copies.append(copy)
    for copy in copies:
        copy.wait()


def stream(packed, partner, extras, weights, sent):
    vmem = pl.BlockSpec(memory_space=pltpu.VMEM)
    return pl.pallas_call(
        stream_kernel,
        out_shape=jax.ShapeDtypeStruct((64, 96, 128), BF16),
        in_specs=[vmem, vmem, vmem, vmem, pl.BlockSpec(memory_space=pl.ANY)],
        out_specs=pl.BlockSpec(memory_space=pl.ANY),
        scratch_shapes=[pltpu.VMEM((64, 48, 128), BF16), pltpu.SemaphoreType.DMA((4,))],
        input_output_aliases={4: 0},
        compiler_params=pltpu.CompilerParams(vmem_limit_bytes=24 * MIB),
    )(packed, partner, extras, weights, sent)


def unpack_kernel(recv, out_x, out_y, sems):
    copies = []
    for which, out in enumerate((out_x, out_y)):
        for c in range(3):
            for run in range(8):
                copies.append(
                    pltpu.make_async_copy(
                        recv.at[pl.ds(8 * COL.index(run), 8), pl.ds(48 * which + 16 * c, 16), :],
                        out.at[c, pl.ds(8 * run, 8)],
                        sems.at[3 * which + c, run],
                    )
                )
    for copy in copies:
        copy.start()
    for copy in copies:
        copy.wait()


def unpack(recv):
    shape = jax.ShapeDtypeStruct((3, 64, 16, 128), BF16)
    anywhere = pl.BlockSpec(memory_space=pl.ANY)
    return pl.pallas_call(
        unpack_kernel,
        out_shape=(shape, shape),
        in_specs=[anywhere],
        out_specs=(anywhere, anywhere),
        scratch_shapes=[pltpu.SemaphoreType.DMA((6, 8))],
        compiler_params=pltpu.CompilerParams(vmem_limit_bytes=16 * MIB),
    )(recv)


def local(velocity, lengths, inverse_x, inverse_y, metric):
    rank = lax.axis_index("row")
    where = jnp.stack([lax.shift_right_logical(rank, 1), rank & 1]).astype(jnp.int32)
    sent = pack(velocity[:, 0], inverse_x)
    weights = build_weights(where, inverse_x, inverse_y, metric.reshape(8, 128))
    received = lax.all_to_all(
        sent, "row", split_axis=0, concat_axis=0, tiled=True, axis_index_groups=[list(ROW)]
    )
    received, (weights_y, weights_x) = lax.optimization_barrier((received, weights))
    packed, extras = compact(lengths, received)
    partner = lax.ppermute(packed, "row", [(i, i ^ 1) for i in range(8)])
    result = normal(packed, weights_y)
    result = stream(packed, partner, extras, weights_x, result)
    moved = lax.all_to_all(
        result,
        "col",
        split_axis=0,
        concat_axis=0,
        tiled=True,
        axis_index_groups=[[8 * run + i for run in COL for i in range(8)]],
    )
    return unpack(moved)


def solution(mesh):
    return jax.shard_map(
        local,
        mesh=mesh,
        in_specs=(P(None, "col", "row", None), P("col", None), P(), P(), P()),
        out_specs=(P(None, None, "col", "row"), P(None, None, "col", "row")),
        check_vma=False,
    )
```

```python
import jax
import jax.numpy as jnp
from jax import lax
from jax.experimental import pallas as pl
from jax.experimental.pallas import tpu as pltpu
from jax.sharding import PartitionSpec as P

A2 = 14.0 / 9.0 / 2.0
B4 = 1.0 / 9.0 / 4.0
ALPHA = 1.0 / 3.0
F32 = jnp.float32
BF16 = jnp.bfloat16
NT = (((1,), (1,)), ((), ()))
MIB = 1 << 20
fixed = pltpu.with_memory_space_constraint
ROW = (5, 4, 1, 0, 7, 6, 3, 2)
COL = (7, 6, 5, 4, 3, 2, 1, 0)
SPANS = ((0, 48), (48, 48), (96, 64))


def lanes(shape):
    return lax.broadcasted_iota(jnp.int32, shape, len(shape) - 1)


def sublanes(shape):
    return lax.broadcasted_iota(jnp.int32, shape, len(shape) - 2)


def split(value):
    high = value.astype(BF16)
    return high, (value - high.astype(F32)).astype(BF16)


def roll(value, shift):
    return pltpu.roll(value, shift % value.shape[-1], value.ndim - 1)


def stencil(rows):
    return A2 * (roll(rows, 1) - roll(rows, -1)) + B4 * (roll(rows, 2) - roll(rows, -2))


def stencil_line(rows):
    width = rows.shape[-1]
    lane = lanes(rows.shape)

    def shifted(by):
        inside = lane >= by if by > 0 else lane < width + by
        return jnp.where(inside, roll(rows, by), 0.0)

    return A2 * (shifted(1) - shifted(-1)) + B4 * (shifted(2) - shifted(-2))


def coupling_rows(first, last, blocks, width):
    total = blocks * width

    def place(row, k):
        parts = []
        if k:
            parts.append(jnp.zeros((1, k * width), F32))
        parts.append(row)
        if k < blocks - 1:
            parts.append(jnp.zeros((1, (blocks - 1 - k) * width), F32))
        return jnp.concatenate(parts, axis=1)

    stacked = jnp.concatenate(
        [place(last[k], k) for k in range(blocks)] + [place(first[k], k) for k in range(blocks)], axis=0
    )
    applied = stencil_line(stacked)
    g_last = []
    for k in range(blocks):
        row = applied[k : k + 1]
        if k:
            row = row - ALPHA * last[k][:, 0:1] * g_last[k - 1]
        g_last.append(row)
    u_first = [None] * blocks
    for k in range(blocks - 1, -1, -1):
        row = applied[blocks + k : blocks + k + 1]
        if k:
            row = row - ALPHA * first[k][:, 0:1] * g_last[k - 1]
        if k < blocks - 1:
            row = row - ALPHA * first[k][:, width - 1 : width] * u_first[k + 1]
        u_first[k] = row
    return g_last, u_first


def functionals(first, last, blocks, width):
    line = blocks * width
    g_last, u_first = coupling_rows(first, last, blocks, width)
    lane = lanes((1, line))
    zero = jnp.zeros((1, line), F32)

    def unit(at):
        return jnp.where(lane == at, 1.0, 0.0)

    rows = []
    for k in range(blocks):
        lo, hi = width * k, width * (k + 1)
        before, after, tip, end = zero, zero, zero, zero
        if k:
            before = -A2 * unit(lo - 1) - B4 * unit(lo - 2) - ALPHA * g_last[k - 1]
            tip = unit(lo - 1)
        if k < blocks - 1:
            after = A2 * unit(hi) + B4 * unit(hi + 1) - ALPHA * u_first[k + 1]
            end = unit(hi)
        rows += [before, before, tip, end, after, after, zero, zero]
    return jnp.concatenate(split(jnp.concatenate(rows, axis=0)), axis=0), g_last, u_first


def coded(value):
    count = value.shape[0] // 2
    value = value[0:count] + value[count : 2 * count]
    top = value.astype(BF16).astype(F32)
    place = sublanes(value.shape) % 8
    return jnp.where((place == 1) | (place == 5), value - top, top)


def edge_columns(tile, lane):
    width = tile.shape[1]
    value = jnp.where((lane == 0) | (lane == 1), tile[:, 0:1], 0.0)
    value = jnp.where(lane == 2, -B4 * tile[:, 1:2], value)
    value = jnp.where(lane == 3, B4 * tile[:, width - 2 : width - 1], value)
    return jnp.where((lane == 4) | (lane == 5), tile[:, width - 1 : width], value)


def pack_kernel(vel_hbm, inv, out, vel, heads, tails, codes, sems, sends):
    blocks, width = inv.shape[0], inv.shape[1]
    line = blocks * width
    copy_heads = pltpu.make_async_copy(inv.at[:, pl.ds(0, 16), :], heads, sems.at[0])
    copy_tails = pltpu.make_async_copy(inv.at[:, pl.ds(width - 16, 16), :], tails, sems.at[1])
    copy_heads.start()
    copy_tails.start()
    comps = vel.shape[0]
    loads, copies = [], []
    for c in range(comps):
        for number, (begin, size) in enumerate(SPANS):
            here = (c, pl.ds(begin, size))
            copy = pltpu.make_async_copy(vel_hbm.at[here], vel.at[here], sems.at[2 + len(SPANS) * c + number])
            copy.start()
            loads.append(copy)
    copy_heads.wait()
    copy_tails.wait()
    first = [heads[k, 0:1, :] for k in range(blocks)]
    last = [tails[k, 15:16, :] for k in range(blocks)]
    both, _, _ = functionals(first, last, blocks, width)
    parts = []
    for c in range(comps):
        for copy in loads[len(SPANS) * c : len(SPANS) * (c + 1)]:
            copy.wait()
        for i in range(out.shape[0]):
            copy = pltpu.make_async_copy(
                vel.at[c, :, pl.ds(128 * ROW[i], 128)], out.at[i, pl.ds(160 * c, 160), :], sends.at[c, i]
            )
            copy.start()
            copies.append(copy)
        parts.append(coded(lax.dot_general(both, vel[c, 0:128, :], NT, preferred_element_type=F32)))
    spare = [vel[c, 128:160, :] for c in range(comps)] + [jnp.zeros((32, line), BF16)]
    spare = jnp.concatenate(spare, axis=0)
    parts.append(coded(lax.dot_general(both, spare, NT, preferred_element_type=F32)))
    for k in range(blocks):
        codes[k] = jnp.concatenate([part[8 * k : 8 * k + 8] for part in parts], axis=0).astype(BF16)
    for i in range(out.shape[0]):
        copy = pltpu.make_async_copy(codes.at[ROW[i] // 2], out.at[i, pl.ds(480, 32), :], sends.at[comps, i])
        copy.start()
        copies.append(copy)
    for copy in copies:
        copy.wait()


def pack(velocity, inverse_x):
    comps, slots, line = velocity.shape
    blocks, width, _ = inverse_x.shape
    return pl.pallas_call(
        pack_kernel,
        out_shape=jax.ShapeDtypeStruct((line // 128, 512, 128), BF16),
        in_specs=[pl.BlockSpec(memory_space=pltpu.HBM), pl.BlockSpec(memory_space=pltpu.HBM)],
        out_specs=pl.BlockSpec(memory_space=pl.ANY),
        scratch_shapes=[
            pltpu.VMEM(velocity.shape, BF16),
            pltpu.VMEM((blocks, 16, width), F32),
            pltpu.VMEM((blocks, 16, width), F32),
            pltpu.VMEM((blocks, 32, 128), BF16),
            pltpu.SemaphoreType.DMA((2 + len(SPANS) * comps,)),
            pltpu.SemaphoreType.DMA((comps + 1, line // 128)),
        ],
        compiler_params=pltpu.CompilerParams(vmem_limit_bytes=24 * MIB),
    )(fixed(velocity, pltpu.HBM), fixed(inverse_x, pltpu.HBM))


def weights_kernel(where, inv_x, inv_y, metric, out_y, out_f, out_x, own, sem):
    blocks, width = inv_y.shape[0], inv_y.shape[1]
    copy = pltpu.make_async_copy(inv_x.at[where[0], pl.ds(where[1] * 128, 128), :], own, sem)
    copy.start()
    first = [inv_y[k, 0:1, :] for k in range(blocks)]
    last = [inv_y[k, width - 1 : width, :] for k in range(blocks)]
    out_f[...], _, _ = functionals(first, last, blocks, width)
    side = jnp.zeros((128, 128), F32)
    lane = lanes((128, 128))
    for k in range(blocks):
        for half in range(width // 128):
            tile = inv_y[k, 128 * half : 128 * half + 128, :]
            inner = stencil(jnp.concatenate([side, tile, side], axis=1))[:, 128 : 128 + width]
            at = k * width + 128 * half
            scale = jnp.broadcast_to(metric[at // 128 : at // 128 + 1, :], (128, 128)).T
            full = jnp.concatenate([inner, edge_columns(tile, lane)], axis=1)
            full = full * jnp.concatenate([scale] * (full.shape[1] // 128), axis=1)
            out_y[0, at : at + 128, :], out_y[1, at : at + 128, :] = split(full)
    copy.wait()
    tile = own[...]
    inner = stencil(jnp.concatenate([side, tile, side], axis=1))
    left, right = inner[:, 128:256], inner[:, 256:384]
    flip = where[1] == 0
    parts = [jnp.where(flip, left, right), jnp.where(flip, right, left)]
    for c in range(3):
        parts.append(edge_columns(tile, lane - 8 * c))
    out_x[0:128, :], out_x[128:256, :] = split(jnp.concatenate(parts, axis=1))


def build_weights(where, inverse_x, inverse_y, metric):
    blocks, width, _ = inverse_y.shape
    size = blocks * width
    vmem = pl.BlockSpec(memory_space=pltpu.VMEM)
    return pl.pallas_call(
        weights_kernel,
        out_shape=(
            jax.ShapeDtypeStruct((2, size, width + 128), BF16),
            jax.ShapeDtypeStruct((16 * blocks, size), BF16),
            jax.ShapeDtypeStruct((256, 640), BF16),
        ),
        in_specs=[pl.BlockSpec(memory_space=pltpu.SMEM), pl.BlockSpec(memory_space=pl.ANY), vmem, vmem],
        out_specs=(vmem, vmem, vmem),
        scratch_shapes=[pltpu.VMEM((128, width), F32), pltpu.SemaphoreType.DMA],
        compiler_params=pltpu.CompilerParams(vmem_limit_bytes=24 * MIB),
        cost_estimate=pl.CostEstimate(flops=20_000_000, bytes_accessed=6_000_000, transcendentals=0),
    )(where, inverse_x, inverse_y, metric)


def target_rows(lengths):
    starts, total = [], jnp.int32(0)
    for s in range(8):
        starts.append(total)
        total = total + lengths[0, s]
    targets = []
    lane = lanes((1, 256))
    for tile in range(5):
        if tile < 4:
            slot, source, names = lane % 128, lane // 128 + 2 * tile, (2 * tile, 2 * tile + 1)
        else:
            slot, source, names = 128 + lane % 32, lane // 32, range(8)
        target = jnp.full((1, 256), -1, jnp.int32)
        for s in names:
            held = (source == s) & (slot < lengths[0, ROW[s]])
            target = jnp.where(held, starts[ROW[s]] + slot, target)
        targets.append(target)
    return jnp.concatenate(targets, axis=1)


def picks(targets, part):
    row = sublanes((256, 1280)) + 256 * part
    return jnp.where(row == targets, 1.0, 0.0).astype(BF16)


def compact_kernel(lengths, recv, weights_hbm, rows_hbm, packed, extras, weights, rows, sems):
    fetches = (
        pltpu.make_async_copy(rows_hbm, rows, sems.at[0]),
        pltpu.make_async_copy(weights_hbm, weights, sems.at[1]),
    )
    for fetch in fetches:
        fetch.start()
    targets = target_rows(lengths)
    small = lanes((8, 128)) // 32
    pad = jnp.zeros((104, 256), F32)
    sent = [recv[s, 480:512, :].astype(F32) for s in range(8)]
    feats = []
    for tile in range(5):
        if tile < 4:
            block = jnp.concatenate([sent[2 * tile][0:24], sent[2 * tile + 1][0:24]], axis=1)
        else:
            halves = []
            for begin in (0, 4):
                lines = []
                for c in range(3):
                    value = jnp.zeros((8, 128), F32)
                    for q in range(4):
                        value = jnp.where(small == q, roll(sent[begin + q][24:32], 32 * (q - c)), value)
                    lines.append(value)
                halves.append(jnp.concatenate(lines, axis=0))
            block = jnp.concatenate(halves, axis=1)
        feats.append(jnp.concatenate([block, pad], axis=0).T.astype(BF16))
    data = []
    for tile in range(5):
        columns = []
        for c in range(3):
            if tile < 4:
                block = recv[2 * tile : 2 * tile + 2, 160 * c : 160 * c + 128, :]
            else:
                block = recv[:, 160 * c + 128 : 160 * c + 160, :]
            columns.append(block.reshape(256, 128))
        data.append(jnp.concatenate(columns + [feats[tile]], axis=1))
    data = jnp.concatenate(data, axis=0)
    for part in range(4):
        here = slice(256 * part, 256 * part + 256)
        value = jnp.dot(picks(targets, part), data, preferred_element_type=F32).astype(BF16)
        packed[here, :] = value[:, 0:384]
        extras[here, :] = value[:, 384:512]
    for fetch in fetches:
        fetch.wait()


def compact(lengths, recv, weights, rows):
    vmem, hbm = pl.BlockSpec(memory_space=pltpu.VMEM), pl.BlockSpec(memory_space=pltpu.HBM)
    return pl.pallas_call(
        compact_kernel,
        out_shape=(
            jax.ShapeDtypeStruct((1024, 384), BF16),
            jax.ShapeDtypeStruct((1024, 128), BF16),
            jax.ShapeDtypeStruct(weights.shape, BF16),
            jax.ShapeDtypeStruct(rows.shape, BF16),
        ),
        in_specs=[pl.BlockSpec(memory_space=pltpu.SMEM), vmem, hbm, hbm],
        out_specs=(vmem, vmem, vmem, vmem),
        scratch_shapes=[pltpu.SemaphoreType.DMA((2,))],
        compiler_params=pltpu.CompilerParams(vmem_limit_bytes=24 * MIB),
    )(lengths, recv, fixed(weights, pltpu.HBM), fixed(rows, pltpu.HBM))


def normal_kernel(packed, weights, rows, out, held, sems):
    field = packed[...]
    edges = coded(jnp.dot(rows[...], field, preferred_element_type=F32))
    spare = jnp.zeros((120, edges.shape[1]), F32)
    copies = []
    for part in range(4):
        here = slice(256 * part, 256 * part + 256)
        edge = jnp.concatenate([edges[8 * part : 8 * part + 8], spare], axis=0).astype(BF16)
        block = jnp.concatenate([field[here], edge], axis=0)
        value = jnp.dot(weights[0, here, :], block, preferred_element_type=F32)
        value = value + jnp.dot(weights[1, here, :], block, preferred_element_type=F32)
        for c in range(3):
            block = value[:, 128 * c : 128 * c + 128].astype(BF16).reshape(16, 16, 128)
            for half in range(2):
                at = 8 * COL.index(2 * part + half)
                held[at : at + 8, 16 * c : 16 * c + 16, :] = block[8 * half : 8 * half + 8]
        for half in range(2):
            runs = pl.ds(8 * COL.index(2 * part + half), 8)
            copy = pltpu.make_async_copy(
                held.at[runs], out.at[runs, pl.ds(48, 48), :], sems.at[2 * part + half]
            )
            copy.start()
            copies.append(copy)
    for copy in copies:
        copy.wait()


def normal(packed, weights, rows):
    vmem = pl.BlockSpec(memory_space=pltpu.VMEM)
    return pl.pallas_call(
        normal_kernel,
        out_shape=jax.ShapeDtypeStruct((64, 96, 128), BF16),
        in_specs=[vmem, vmem, vmem],
        out_specs=pl.BlockSpec(memory_space=pl.ANY),
        scratch_shapes=[pltpu.VMEM((64, 48, 128), BF16), pltpu.SemaphoreType.DMA((8,))],
        compiler_params=pltpu.CompilerParams(vmem_limit_bytes=24 * MIB),
        cost_estimate=pl.CostEstimate(flops=1_600_000_000, bytes_accessed=6_000_000, transcendentals=0),
    )(packed, weights, rows)


def stream_kernel(packed, partner, extras, weights, sent, out, held, sems):
    del sent
    copies = []
    for c in range(3):
        columns = slice(128 * c, 128 * c + 128)
        field = jnp.concatenate([packed[:, columns], partner[:, columns], extras[...]], axis=1)
        matrix = jnp.concatenate(
            [weights[:, 0:256], weights[:, 256 + 128 * c : 384 + 128 * c]], axis=1
        )
        value = lax.dot_general(field, matrix, NT, preferred_element_type=F32)
        value = value[:, 0:128] + value[:, 128:256]
        rows = pl.ds(16 * c, 16)
        block = value.astype(BF16).reshape(64, 16, 128)
        for run in range(8):
            at = 8 * COL.index(run)
            held[at : at + 8, 16 * c : 16 * c + 16, :] = block[8 * run : 8 * run + 8]
        copy = pltpu.make_async_copy(held.at[:, rows, :], out.at[:, rows, :], sems.at[c])
        copy.start()
        copies.append(copy)
    for copy in copies:
        copy.wait()


def stream(packed, partner, extras, weights, sent):
    vmem = pl.BlockSpec(memory_space=pltpu.VMEM)
    return pl.pallas_call(
        stream_kernel,
        out_shape=jax.ShapeDtypeStruct((64, 96, 128), BF16),
        in_specs=[vmem, vmem, vmem, vmem, pl.BlockSpec(memory_space=pl.ANY)],
        out_specs=pl.BlockSpec(memory_space=pl.ANY),
        scratch_shapes=[pltpu.VMEM((64, 48, 128), BF16), pltpu.SemaphoreType.DMA((4,))],
        input_output_aliases={4: 0},
        compiler_params=pltpu.CompilerParams(vmem_limit_bytes=24 * MIB),
    )(packed, partner, extras, weights, sent)


def unpack_kernel(recv, out_x, out_y, sems):
    copies = []
    for which, out in enumerate((out_x, out_y)):
        for c in range(3):
            for run in range(8):
                copies.append(
                    pltpu.make_async_copy(
                        recv.at[pl.ds(8 * COL.index(run), 8), pl.ds(48 * which + 16 * c, 16), :],
                        out.at[c, pl.ds(8 * run, 8)],
                        sems.at[3 * which + c, run],
                    )
                )
    for copy in copies:
        copy.start()
    for copy in copies:
        copy.wait()


def unpack(recv):
    shape = jax.ShapeDtypeStruct((3, 64, 16, 128), BF16)
    anywhere = pl.BlockSpec(memory_space=pl.ANY)
    return pl.pallas_call(
        unpack_kernel,
        out_shape=(shape, shape),
        in_specs=[anywhere],
        out_specs=(anywhere, anywhere),
        scratch_shapes=[pltpu.SemaphoreType.DMA((6, 8))],
        compiler_params=pltpu.CompilerParams(vmem_limit_bytes=16 * MIB),
    )(recv)


def local(velocity, lengths, inverse_x, inverse_y, metric):
    rank = lax.axis_index("row")
    where = jnp.stack([lax.shift_right_logical(rank, 1), rank & 1]).astype(jnp.int32)
    sent = pack(velocity[:, 0], inverse_x)
    weights = build_weights(where, inverse_x, inverse_y, metric.reshape(8, 128))
    received = lax.all_to_all(
        sent, "row", split_axis=0, concat_axis=0, tiled=True, axis_index_groups=[list(ROW)]
    )
    received, (weights_y, rows, weights_x) = lax.optimization_barrier((received, weights))
    packed, extras, weights_y, rows = compact(lengths, received, weights_y, rows)
    partner = lax.ppermute(packed, "row", [(i, i ^ 1) for i in range(8)])
    result = normal(packed, weights_y, rows)
    result = stream(packed, partner, extras, weights_x, result)
    moved = lax.all_to_all(
        result,
        "col",
        split_axis=0,
        concat_axis=0,
        tiled=True,
        axis_index_groups=[[8 * run + i for run in COL for i in range(8)]],
    )
    return unpack(moved)


def solution(mesh):
    return jax.shard_map(
        local,
        mesh=mesh,
        in_specs=(P(None, "col", "row", None), P("col", None), P(), P(), P()),
        out_specs=(P(None, None, "col", "row"), P(None, None, "col", "row")),
        check_vma=False,
    )
```

```python
import jax
import jax.numpy as jnp
from jax import lax
from jax.experimental import pallas as pl
from jax.experimental.pallas import tpu as pltpu
from jax.sharding import PartitionSpec as P

A2 = 14.0 / 9.0 / 2.0
B4 = 1.0 / 9.0 / 4.0
ALPHA = 1.0 / 3.0
F32 = jnp.float32
BF16 = jnp.bfloat16
NT = (((1,), (1,)), ((), ()))
MIB = 1 << 20
fixed = pltpu.with_memory_space_constraint
ROW = (5, 4, 1, 0, 7, 6, 3, 2)
COL = (7, 6, 5, 4, 3, 2, 1, 0)
SPANS = ((0, 160),)


def lanes(shape):
    return lax.broadcasted_iota(jnp.int32, shape, len(shape) - 1)


def sublanes(shape):
    return lax.broadcasted_iota(jnp.int32, shape, len(shape) - 2)


def split(value):
    high = value.astype(BF16)
    return high, (value - high.astype(F32)).astype(BF16)


def roll(value, shift):
    return pltpu.roll(value, shift % value.shape[-1], value.ndim - 1)


def stencil(rows):
    return A2 * (roll(rows, 1) - roll(rows, -1)) + B4 * (roll(rows, 2) - roll(rows, -2))


def stencil_line(rows):
    width = rows.shape[-1]
    lane = lanes(rows.shape)

    def shifted(by):
        inside = lane >= by if by > 0 else lane < width + by
        return jnp.where(inside, roll(rows, by), 0.0)

    return A2 * (shifted(1) - shifted(-1)) + B4 * (shifted(2) - shifted(-2))


def coupling_rows(first, last, blocks, width):
    total = blocks * width

    def place(row, k):
        parts = []
        if k:
            parts.append(jnp.zeros((1, k * width), F32))
        parts.append(row)
        if k < blocks - 1:
            parts.append(jnp.zeros((1, (blocks - 1 - k) * width), F32))
        return jnp.concatenate(parts, axis=1)

    stacked = jnp.concatenate(
        [place(last[k], k) for k in range(blocks)] + [place(first[k], k) for k in range(blocks)], axis=0
    )
    applied = stencil_line(stacked)
    g_last = []
    for k in range(blocks):
        row = applied[k : k + 1]
        if k:
            row = row - ALPHA * last[k][:, 0:1] * g_last[k - 1]
        g_last.append(row)
    u_first = [None] * blocks
    for k in range(blocks - 1, -1, -1):
        row = applied[blocks + k : blocks + k + 1]
        if k:
            row = row - ALPHA * first[k][:, 0:1] * g_last[k - 1]
        if k < blocks - 1:
            row = row - ALPHA * first[k][:, width - 1 : width] * u_first[k + 1]
        u_first[k] = row
    return g_last, u_first


def functionals(first, last, blocks, width):
    line = blocks * width
    g_last, u_first = coupling_rows(first, last, blocks, width)
    lane = lanes((1, line))
    zero = jnp.zeros((1, line), F32)

    def unit(at):
        return jnp.where(lane == at, 1.0, 0.0)

    rows = []
    for k in range(blocks):
        lo, hi = width * k, width * (k + 1)
        before, after, tip, end = zero, zero, zero, zero
        if k:
            before = -A2 * unit(lo - 1) - B4 * unit(lo - 2) - ALPHA * g_last[k - 1]
            tip = unit(lo - 1)
        if k < blocks - 1:
            after = A2 * unit(hi) + B4 * unit(hi + 1) - ALPHA * u_first[k + 1]
            end = unit(hi)
        rows += [before, before, tip, end, after, after, zero, zero]
    return jnp.concatenate(split(jnp.concatenate(rows, axis=0)), axis=0), g_last, u_first


def coded(value):
    count = value.shape[0] // 2
    value = value[0:count] + value[count : 2 * count]
    top = value.astype(BF16).astype(F32)
    place = sublanes(value.shape) % 8
    return jnp.where((place == 1) | (place == 5), value - top, top)


def edge_columns(tile, lane):
    width = tile.shape[1]
    value = jnp.where((lane == 0) | (lane == 1), tile[:, 0:1], 0.0)
    value = jnp.where(lane == 2, -B4 * tile[:, 1:2], value)
    value = jnp.where(lane == 3, B4 * tile[:, width - 2 : width - 1], value)
    return jnp.where((lane == 4) | (lane == 5), tile[:, width - 1 : width], value)


def pack_kernel(vel_hbm, inv, out, vel, heads, tails, codes, sems, sends):
    blocks, width = inv.shape[0], inv.shape[1]
    line = blocks * width
    copy_heads = pltpu.make_async_copy(inv.at[:, pl.ds(0, 16), :], heads, sems.at[0])
    copy_tails = pltpu.make_async_copy(inv.at[:, pl.ds(width - 16, 16), :], tails, sems.at[1])
    copy_heads.start()
    copy_tails.start()
    comps = vel.shape[0]
    loads, copies = [], []
    for c in range(comps):
        for number, (begin, size) in enumerate(SPANS):
            here = (c, pl.ds(begin, size))
            copy = pltpu.make_async_copy(vel_hbm.at[here], vel.at[here], sems.at[2 + len(SPANS) * c + number])
            copy.start()
            loads.append(copy)
    copy_heads.wait()
    copy_tails.wait()
    first = [heads[k, 0:1, :] for k in range(blocks)]
    last = [tails[k, 15:16, :] for k in range(blocks)]
    both, _, _ = functionals(first, last, blocks, width)
    parts = []
    for c in range(comps):
        for copy in loads[len(SPANS) * c : len(SPANS) * (c + 1)]:
            copy.wait()
        for i in range(out.shape[0]):
            copy = pltpu.make_async_copy(
                vel.at[c, :, pl.ds(128 * ROW[i], 128)], out.at[i, pl.ds(160 * c, 160), :], sends.at[c, i]
            )
            copy.start()
            copies.append(copy)
        parts.append(coded(lax.dot_general(both, vel[c, 0:128, :], NT, preferred_element_type=F32)))
    spare = [vel[c, 128:160, :] for c in range(comps)] + [jnp.zeros((32, line), BF16)]
    spare = jnp.concatenate(spare, axis=0)
    parts.append(coded(lax.dot_general(both, spare, NT, preferred_element_type=F32)))
    for k in range(blocks):
        codes[k] = jnp.concatenate([part[8 * k : 8 * k + 8] for part in parts], axis=0).astype(BF16)
    for i in range(out.shape[0]):
        copy = pltpu.make_async_copy(codes.at[ROW[i] // 2], out.at[i, pl.ds(480, 32), :], sends.at[comps, i])
        copy.start()
        copies.append(copy)
    for copy in copies:
        copy.wait()


def pack(velocity, inverse_x):
    comps, slots, line = velocity.shape
    blocks, width, _ = inverse_x.shape
    return pl.pallas_call(
        pack_kernel,
        out_shape=jax.ShapeDtypeStruct((line // 128, 512, 128), BF16),
        in_specs=[pl.BlockSpec(memory_space=pltpu.HBM), pl.BlockSpec(memory_space=pltpu.HBM)],
        out_specs=pl.BlockSpec(memory_space=pl.ANY),
        scratch_shapes=[
            pltpu.VMEM(velocity.shape, BF16),
            pltpu.VMEM((blocks, 16, width), F32),
            pltpu.VMEM((blocks, 16, width), F32),
            pltpu.VMEM((blocks, 32, 128), BF16),
            pltpu.SemaphoreType.DMA((2 + len(SPANS) * comps,)),
            pltpu.SemaphoreType.DMA((comps + 1, line // 128)),
        ],
        compiler_params=pltpu.CompilerParams(vmem_limit_bytes=24 * MIB),
    )(fixed(velocity, pltpu.HBM), fixed(inverse_x, pltpu.HBM))


def weights_kernel(where, inv_x, inv_y, metric, out_y, out_f, out_x, own, sem):
    blocks, width = inv_y.shape[0], inv_y.shape[1]
    copy = pltpu.make_async_copy(inv_x.at[where[0], pl.ds(where[1] * 128, 128), :], own, sem)
    copy.start()
    first = [inv_y[k, 0:1, :] for k in range(blocks)]
    last = [inv_y[k, width - 1 : width, :] for k in range(blocks)]
    out_f[...], _, _ = functionals(first, last, blocks, width)
    side = jnp.zeros((128, 128), F32)
    lane = lanes((128, 128))
    for k in range(blocks):
        for half in range(width // 128):
            tile = inv_y[k, 128 * half : 128 * half + 128, :]
            inner = stencil(jnp.concatenate([side, tile, side], axis=1))[:, 128 : 128 + width]
            at = k * width + 128 * half
            scale = jnp.broadcast_to(metric[at // 128 : at // 128 + 1, :], (128, 128)).T
            full = jnp.concatenate([inner, edge_columns(tile, lane)], axis=1)
            full = full * jnp.concatenate([scale] * (full.shape[1] // 128), axis=1)
            out_y[0, at : at + 128, :], out_y[1, at : at + 128, :] = split(full)
    copy.wait()
    tile = own[...]
    inner = stencil(jnp.concatenate([side, tile, side], axis=1))
    left, right = inner[:, 128:256], inner[:, 256:384]
    flip = where[1] == 0
    parts = [jnp.where(flip, left, right), jnp.where(flip, right, left)]
    for c in range(3):
        parts.append(edge_columns(tile, lane - 8 * c))
    out_x[0:128, :], out_x[128:256, :] = split(jnp.concatenate(parts, axis=1))


def build_weights(where, inverse_x, inverse_y, metric):
    blocks, width, _ = inverse_y.shape
    size = blocks * width
    vmem = pl.BlockSpec(memory_space=pltpu.VMEM)
    return pl.pallas_call(
        weights_kernel,
        out_shape=(
            jax.ShapeDtypeStruct((2, size, width + 128), BF16),
            jax.ShapeDtypeStruct((16 * blocks, size), BF16),
            jax.ShapeDtypeStruct((256, 640), BF16),
        ),
        in_specs=[pl.BlockSpec(memory_space=pltpu.SMEM), pl.BlockSpec(memory_space=pl.ANY), vmem, vmem],
        out_specs=(vmem, vmem, vmem),
        scratch_shapes=[pltpu.VMEM((128, width), F32), pltpu.SemaphoreType.DMA],
        compiler_params=pltpu.CompilerParams(vmem_limit_bytes=24 * MIB),
        cost_estimate=pl.CostEstimate(flops=20_000_000, bytes_accessed=6_000_000, transcendentals=0),
    )(where, inverse_x, inverse_y, metric)


def target_rows(lengths):
    starts, total = [], jnp.int32(0)
    for s in range(8):
        starts.append(total)
        total = total + lengths[0, s]
    targets = []
    lane = lanes((1, 256))
    for tile in range(5):
        if tile < 4:
            slot, source, names = lane % 128, lane // 128 + 2 * tile, (2 * tile, 2 * tile + 1)
        else:
            slot, source, names = 128 + lane % 32, lane // 32, range(8)
        target = jnp.full((1, 256), -1, jnp.int32)
        for s in names:
            held = (source == s) & (slot < lengths[0, ROW[s]])
            target = jnp.where(held, starts[ROW[s]] + slot, target)
        targets.append(target)
    return jnp.concatenate(targets, axis=1)


def picks(targets, part):
    row = sublanes((256, 1280)) + 256 * part
    return jnp.where(row == targets, 1.0, 0.0).astype(BF16)


def compact_kernel(lengths, recv, weights_hbm, rows_hbm, packed, extras, weights, rows, sems):
    fetches = (
        pltpu.make_async_copy(rows_hbm, rows, sems.at[0]),
        pltpu.make_async_copy(weights_hbm, weights, sems.at[1]),
    )
    for fetch in fetches:
        fetch.start()
    targets = target_rows(lengths)
    small = lanes((8, 128)) // 32
    pad = jnp.zeros((104, 256), F32)
    sent = [recv[s, 480:512, :].astype(F32) for s in range(8)]
    feats = []
    for tile in range(5):
        if tile < 4:
            block = jnp.concatenate([sent[2 * tile][0:24], sent[2 * tile + 1][0:24]], axis=1)
        else:
            halves = []
            for begin in (0, 4):
                lines = []
                for c in range(3):
                    value = jnp.zeros((8, 128), F32)
                    for q in range(4):
                        value = jnp.where(small == q, roll(sent[begin + q][24:32], 32 * (q - c)), value)
                    lines.append(value)
                halves.append(jnp.concatenate(lines, axis=0))
            block = jnp.concatenate(halves, axis=1)
        feats.append(jnp.concatenate([block, pad], axis=0).T.astype(BF16))
    data = []
    for tile in range(5):
        columns = []
        for c in range(3):
            if tile < 4:
                block = recv[2 * tile : 2 * tile + 2, 160 * c : 160 * c + 128, :]
            else:
                block = recv[:, 160 * c + 128 : 160 * c + 160, :]
            columns.append(block.reshape(256, 128))
        data.append(jnp.concatenate(columns + [feats[tile]], axis=1))
    data = jnp.concatenate(data, axis=0)
    for part in range(4):
        here = slice(256 * part, 256 * part + 256)
        value = jnp.dot(picks(targets, part), data, preferred_element_type=F32).astype(BF16)
        packed[here, :] = value[:, 0:384]
        extras[here, :] = value[:, 384:512]
    for fetch in fetches:
        fetch.wait()


def compact(lengths, recv, weights, rows):
    vmem, hbm = pl.BlockSpec(memory_space=pltpu.VMEM), pl.BlockSpec(memory_space=pltpu.HBM)
    return pl.pallas_call(
        compact_kernel,
        out_shape=(
            jax.ShapeDtypeStruct((1024, 384), BF16),
            jax.ShapeDtypeStruct((1024, 128), BF16),
            jax.ShapeDtypeStruct(weights.shape, BF16),
            jax.ShapeDtypeStruct(rows.shape, BF16),
        ),
        in_specs=[pl.BlockSpec(memory_space=pltpu.SMEM), vmem, hbm, hbm],
        out_specs=(vmem, vmem, vmem, vmem),
        scratch_shapes=[pltpu.SemaphoreType.DMA((2,))],
        compiler_params=pltpu.CompilerParams(vmem_limit_bytes=24 * MIB),
    )(lengths, recv, fixed(weights, pltpu.HBM), fixed(rows, pltpu.HBM))


def normal_kernel(packed, weights, rows, out):
    field = packed[...]
    edges = coded(jnp.dot(rows[...], field, preferred_element_type=F32))
    spare = jnp.zeros((120, edges.shape[1]), F32)
    for part in range(4):
        here = slice(256 * part, 256 * part + 256)
        edge = jnp.concatenate([edges[8 * part : 8 * part + 8], spare], axis=0).astype(BF16)
        block = jnp.concatenate([field[here], edge], axis=0)
        value = jnp.dot(weights[0, here, :], block, preferred_element_type=F32)
        value = value + jnp.dot(weights[1, here, :], block, preferred_element_type=F32)
        for c in range(3):
            block = value[:, 128 * c : 128 * c + 128].astype(BF16).reshape(16, 16, 128)
            for half in range(2):
                at = 8 * COL.index(2 * part + half)
                out[at : at + 8, 16 * c : 16 * c + 16, :] = block[8 * half : 8 * half + 8]


def normal(packed, weights, rows):
    vmem = pl.BlockSpec(memory_space=pltpu.VMEM)
    return pl.pallas_call(
        normal_kernel,
        out_shape=jax.ShapeDtypeStruct((64, 48, 128), BF16),
        in_specs=[vmem, vmem, vmem],
        out_specs=vmem,
        compiler_params=pltpu.CompilerParams(vmem_limit_bytes=24 * MIB),
        cost_estimate=pl.CostEstimate(flops=1_600_000_000, bytes_accessed=6_000_000, transcendentals=0),
    )(packed, weights, rows)


def stream_kernel(packed, partner, extras, weights, sent, out):
    for c in range(3):
        columns = slice(128 * c, 128 * c + 128)
        field = jnp.concatenate([packed[:, columns], partner[:, columns], extras[...]], axis=1)
        matrix = jnp.concatenate(
            [weights[:, 0:256], weights[:, 256 + 128 * c : 384 + 128 * c]], axis=1
        )
        value = lax.dot_general(field, matrix, NT, preferred_element_type=F32)
        value = value[:, 0:128] + value[:, 128:256]
        block = value.astype(BF16).reshape(64, 16, 128)
        for run in range(8):
            at = 8 * COL.index(run)
            out[at : at + 8, 16 * c : 16 * c + 16, :] = block[8 * run : 8 * run + 8]
        out[:, 48 + 16 * c : 64 + 16 * c, :] = sent[:, 16 * c : 16 * c + 16, :]


def stream(packed, partner, extras, weights, sent):
    vmem = pl.BlockSpec(memory_space=pltpu.VMEM)
    return pl.pallas_call(
        stream_kernel,
        out_shape=jax.ShapeDtypeStruct((64, 96, 128), BF16),
        in_specs=[vmem] * 5,
        out_specs=vmem,
        compiler_params=pltpu.CompilerParams(vmem_limit_bytes=24 * MIB),
    )(packed, partner, extras, weights, sent)


def unpack_kernel(recv, out_x, out_y, held, sems):
    copies = []
    for which, out in enumerate((out_x, out_y)):
        for c in range(3):
            at = 48 * which + 16 * c
            for run in range(8):
                begin = 8 * COL.index(run)
                held[which, c, 8 * run : 8 * run + 8] = recv[begin : begin + 8, at : at + 16, :]
            copy = pltpu.make_async_copy(held.at[which, c], out.at[c], sems.at[3 * which + c])
            copy.start()
            copies.append(copy)
    for copy in copies:
        copy.wait()


def unpack(recv):
    shape = jax.ShapeDtypeStruct((3, 64, 16, 128), BF16)
    anywhere = pl.BlockSpec(memory_space=pl.ANY)
    return pl.pallas_call(
        unpack_kernel,
        out_shape=(shape, shape),
        in_specs=[pl.BlockSpec(memory_space=pltpu.VMEM)],
        out_specs=(anywhere, anywhere),
        scratch_shapes=[pltpu.VMEM((2, 3, 64, 16, 128), BF16), pltpu.SemaphoreType.DMA((6,))],
        compiler_params=pltpu.CompilerParams(vmem_limit_bytes=24 * MIB),
    )(recv)


def local(velocity, lengths, inverse_x, inverse_y, metric):
    rank = lax.axis_index("row")
    where = jnp.stack([lax.shift_right_logical(rank, 1), rank & 1]).astype(jnp.int32)
    sent = pack(velocity[:, 0], inverse_x)
    weights = build_weights(where, inverse_x, inverse_y, metric.reshape(8, 128))
    received = lax.all_to_all(
        sent, "row", split_axis=0, concat_axis=0, tiled=True, axis_index_groups=[list(ROW)]
    )
    received, (weights_y, rows, weights_x) = lax.optimization_barrier((received, weights))
    packed, extras, weights_y, rows = compact(lengths, received, weights_y, rows)
    partner = lax.ppermute(packed, "row", [(i, i ^ 1) for i in range(8)])
    result = normal(packed, weights_y, rows)
    result = stream(packed, partner, extras, weights_x, result)
    moved = lax.all_to_all(
        result,
        "col",
        split_axis=0,
        concat_axis=0,
        tiled=True,
        axis_index_groups=[[8 * run + i for run in COL for i in range(8)]],
    )
    return unpack(moved)


def solution(mesh):
    return jax.shard_map(
        local,
        mesh=mesh,
        in_specs=(P(None, "col", "row", None), P("col", None), P(), P(), P()),
        out_specs=(P(None, None, "col", "row"), P(None, None, "col", "row")),
        check_vma=False,
    )
```

```python
import jax
import jax.numpy as jnp
from jax import lax
from jax.experimental import pallas as pl
from jax.experimental.pallas import tpu as pltpu
from jax.sharding import PartitionSpec as P

A2 = 14.0 / 9.0 / 2.0
B4 = 1.0 / 9.0 / 4.0
ALPHA = 1.0 / 3.0
F32 = jnp.float32
BF16 = jnp.bfloat16
NT = (((1,), (1,)), ((), ()))
MIB = 1 << 20
fixed = pltpu.with_memory_space_constraint
ROW = (5, 4, 1, 0, 3, 2, 7, 6)
COL = (7, 6, 5, 4, 3, 2, 1, 0)
SPANS = ((0, 160),)


def lanes(shape):
    return lax.broadcasted_iota(jnp.int32, shape, len(shape) - 1)


def sublanes(shape):
    return lax.broadcasted_iota(jnp.int32, shape, len(shape) - 2)


def split(value):
    high = value.astype(BF16)
    return high, (value - high.astype(F32)).astype(BF16)


def roll(value, shift):
    return pltpu.roll(value, shift % value.shape[-1], value.ndim - 1)


def stencil(rows):
    return A2 * (roll(rows, 1) - roll(rows, -1)) + B4 * (roll(rows, 2) - roll(rows, -2))


def stencil_line(rows):
    width = rows.shape[-1]
    lane = lanes(rows.shape)

    def shifted(by):
        inside = lane >= by if by > 0 else lane < width + by
        return jnp.where(inside, roll(rows, by), 0.0)

    return A2 * (shifted(1) - shifted(-1)) + B4 * (shifted(2) - shifted(-2))


def coupling_rows(first, last, blocks, width):
    total = blocks * width

    def place(row, k):
        parts = []
        if k:
            parts.append(jnp.zeros((1, k * width), F32))
        parts.append(row)
        if k < blocks - 1:
            parts.append(jnp.zeros((1, (blocks - 1 - k) * width), F32))
        return jnp.concatenate(parts, axis=1)

    stacked = jnp.concatenate(
        [place(last[k], k) for k in range(blocks)] + [place(first[k], k) for k in range(blocks)], axis=0
    )
    applied = stencil_line(stacked)
    g_last = []
    for k in range(blocks):
        row = applied[k : k + 1]
        if k:
            row = row - ALPHA * last[k][:, 0:1] * g_last[k - 1]
        g_last.append(row)
    u_first = [None] * blocks
    for k in range(blocks - 1, -1, -1):
        row = applied[blocks + k : blocks + k + 1]
        if k:
            row = row - ALPHA * first[k][:, 0:1] * g_last[k - 1]
        if k < blocks - 1:
            row = row - ALPHA * first[k][:, width - 1 : width] * u_first[k + 1]
        u_first[k] = row
    return g_last, u_first


def functionals(first, last, blocks, width):
    line = blocks * width
    g_last, u_first = coupling_rows(first, last, blocks, width)
    lane = lanes((1, line))
    zero = jnp.zeros((1, line), F32)

    def unit(at):
        return jnp.where(lane == at, 1.0, 0.0)

    rows = []
    for k in range(blocks):
        lo, hi = width * k, width * (k + 1)
        before, after, tip, end = zero, zero, zero, zero
        if k:
            before = -A2 * unit(lo - 1) - B4 * unit(lo - 2) - ALPHA * g_last[k - 1]
            tip = unit(lo - 1)
        if k < blocks - 1:
            after = A2 * unit(hi) + B4 * unit(hi + 1) - ALPHA * u_first[k + 1]
            end = unit(hi)
        rows += [before, before, tip, end, after, after, zero, zero]
    return jnp.concatenate(split(jnp.concatenate(rows, axis=0)), axis=0), g_last, u_first


def coded(value):
    count = value.shape[0] // 2
    value = value[0:count] + value[count : 2 * count]
    top = value.astype(BF16).astype(F32)
    place = sublanes(value.shape) % 8
    return jnp.where((place == 1) | (place == 5), value - top, top)


def edge_columns(tile, lane):
    width = tile.shape[1]
    value = jnp.where((lane == 0) | (lane == 1), tile[:, 0:1], 0.0)
    value = jnp.where(lane == 2, -B4 * tile[:, 1:2], value)
    value = jnp.where(lane == 3, B4 * tile[:, width - 2 : width - 1], value)
    return jnp.where((lane == 4) | (lane == 5), tile[:, width - 1 : width], value)


def pack_kernel(vel_hbm, inv, out, vel, heads, tails, codes, sems, sends):
    blocks, width = inv.shape[0], inv.shape[1]
    line = blocks * width
    copy_heads = pltpu.make_async_copy(inv.at[:, pl.ds(0, 16), :], heads, sems.at[0])
    copy_tails = pltpu.make_async_copy(inv.at[:, pl.ds(width - 16, 16), :], tails, sems.at[1])
    copy_heads.start()
    copy_tails.start()
    comps = vel.shape[0]
    loads, copies = [], []
    for c in range(comps):
        for number, (begin, size) in enumerate(SPANS):
            here = (c, pl.ds(begin, size))
            copy = pltpu.make_async_copy(vel_hbm.at[here], vel.at[here], sems.at[2 + len(SPANS) * c + number])
            copy.start()
            loads.append(copy)
    copy_heads.wait()
    copy_tails.wait()
    first = [heads[k, 0:1, :] for k in range(blocks)]
    last = [tails[k, 15:16, :] for k in range(blocks)]
    both, _, _ = functionals(first, last, blocks, width)
    parts = []
    for c in range(comps):
        for copy in loads[len(SPANS) * c : len(SPANS) * (c + 1)]:
            copy.wait()
        for i in range(out.shape[0]):
            copy = pltpu.make_async_copy(
                vel.at[c, :, pl.ds(128 * ROW[i], 128)], out.at[i, pl.ds(160 * c, 160), :], sends.at[c, i]
            )
            copy.start()
            copies.append(copy)
        parts.append(coded(lax.dot_general(both, vel[c, 0:128, :], NT, preferred_element_type=F32)))
    spare = [vel[c, 128:160, :] for c in range(comps)] + [jnp.zeros((32, line), BF16)]
    spare = jnp.concatenate(spare, axis=0)
    parts.append(coded(lax.dot_general(both, spare, NT, preferred_element_type=F32)))
    for k in range(blocks):
        codes[k] = jnp.concatenate([part[8 * k : 8 * k + 8] for part in parts], axis=0).astype(BF16)
    for i in range(out.shape[0]):
        copy = pltpu.make_async_copy(codes.at[ROW[i] // 2], out.at[i, pl.ds(480, 32), :], sends.at[comps, i])
        copy.start()
        copies.append(copy)
    for copy in copies:
        copy.wait()


def pack(velocity, inverse_x):
    comps, slots, line = velocity.shape
    blocks, width, _ = inverse_x.shape
    return pl.pallas_call(
        pack_kernel,
        out_shape=jax.ShapeDtypeStruct((line // 128, 512, 128), BF16),
        in_specs=[pl.BlockSpec(memory_space=pltpu.HBM), pl.BlockSpec(memory_space=pltpu.HBM)],
        out_specs=pl.BlockSpec(memory_space=pl.ANY),
        scratch_shapes=[
            pltpu.VMEM(velocity.shape, BF16),
            pltpu.VMEM((blocks, 16, width), F32),
            pltpu.VMEM((blocks, 16, width), F32),
            pltpu.VMEM((blocks, 32, 128), BF16),
            pltpu.SemaphoreType.DMA((2 + len(SPANS) * comps,)),
            pltpu.SemaphoreType.DMA((comps + 1, line // 128)),
        ],
        compiler_params=pltpu.CompilerParams(vmem_limit_bytes=24 * MIB),
    )(fixed(velocity, pltpu.HBM), fixed(inverse_x, pltpu.HBM))


def weights_kernel(where, inv_x, inv_y, metric, out_y, out_f, out_x, own, sem):
    blocks, width = inv_y.shape[0], inv_y.shape[1]
    copy = pltpu.make_async_copy(inv_x.at[where[0], pl.ds(where[1] * 128, 128), :], own, sem)
    copy.start()
    first = [inv_y[k, 0:1, :] for k in range(blocks)]
    last = [inv_y[k, width - 1 : width, :] for k in range(blocks)]
    out_f[...], _, _ = functionals(first, last, blocks, width)
    side = jnp.zeros((128, 128), F32)
    lane = lanes((128, 128))
    for k in range(blocks):
        for half in range(width // 128):
            tile = inv_y[k, 128 * half : 128 * half + 128, :]
            inner = stencil(jnp.concatenate([side, tile, side], axis=1))[:, 128 : 128 + width]
            at = k * width + 128 * half
            scale = jnp.broadcast_to(metric[at // 128 : at // 128 + 1, :], (128, 128)).T
            full = jnp.concatenate([inner, edge_columns(tile, lane)], axis=1)
            full = full * jnp.concatenate([scale] * (full.shape[1] // 128), axis=1)
            out_y[0, at : at + 128, :], out_y[1, at : at + 128, :] = split(full)
    copy.wait()
    tile = own[...]
    inner = stencil(jnp.concatenate([side, tile, side], axis=1))
    left, right = inner[:, 128:256], inner[:, 256:384]
    flip = where[1] == 0
    parts = [jnp.where(flip, left, right), jnp.where(flip, right, left)]
    for c in range(3):
        parts.append(edge_columns(tile, lane - 8 * c))
    out_x[0:128, :], out_x[128:256, :] = split(jnp.concatenate(parts, axis=1))


def build_weights(where, inverse_x, inverse_y, metric):
    blocks, width, _ = inverse_y.shape
    size = blocks * width
    vmem = pl.BlockSpec(memory_space=pltpu.VMEM)
    return pl.pallas_call(
        weights_kernel,
        out_shape=(
            jax.ShapeDtypeStruct((2, size, width + 128), BF16),
            jax.ShapeDtypeStruct((16 * blocks, size), BF16),
            jax.ShapeDtypeStruct((256, 640), BF16),
        ),
        in_specs=[pl.BlockSpec(memory_space=pltpu.SMEM), pl.BlockSpec(memory_space=pl.ANY), vmem, vmem],
        out_specs=(vmem, vmem, vmem),
        scratch_shapes=[pltpu.VMEM((128, width), F32), pltpu.SemaphoreType.DMA],
        compiler_params=pltpu.CompilerParams(vmem_limit_bytes=24 * MIB),
        cost_estimate=pl.CostEstimate(flops=20_000_000, bytes_accessed=6_000_000, transcendentals=0),
    )(where, inverse_x, inverse_y, metric)


def target_rows(lengths):
    starts, total = [], jnp.int32(0)
    for s in range(8):
        starts.append(total)
        total = total + lengths[0, s]
    targets = []
    lane = lanes((1, 256))
    for tile in range(5):
        if tile < 4:
            slot, source, names = lane % 128, lane // 128 + 2 * tile, (2 * tile, 2 * tile + 1)
        else:
            slot, source, names = 128 + lane % 32, lane // 32, range(8)
        target = jnp.full((1, 256), -1, jnp.int32)
        for s in names:
            held = (source == s) & (slot < lengths[0, ROW[s]])
            target = jnp.where(held, starts[ROW[s]] + slot, target)
        targets.append(target)
    return jnp.concatenate(targets, axis=1)


def picks(targets, part):
    row = sublanes((256, 1280)) + 256 * part
    return jnp.where(row == targets, 1.0, 0.0).astype(BF16)


def compact_kernel(lengths, recv, weights_hbm, rows_hbm, packed, extras, weights, rows, sems):
    fetches = (
        pltpu.make_async_copy(rows_hbm, rows, sems.at[0]),
        pltpu.make_async_copy(weights_hbm, weights, sems.at[1]),
    )
    for fetch in fetches:
        fetch.start()
    targets = target_rows(lengths)
    small = lanes((8, 128)) // 32
    pad = jnp.zeros((104, 256), F32)
    sent = [recv[s, 480:512, :].astype(F32) for s in range(8)]
    feats = []
    for tile in range(5):
        if tile < 4:
            block = jnp.concatenate([sent[2 * tile][0:24], sent[2 * tile + 1][0:24]], axis=1)
        else:
            halves = []
            for begin in (0, 4):
                lines = []
                for c in range(3):
                    value = jnp.zeros((8, 128), F32)
                    for q in range(4):
                        value = jnp.where(small == q, roll(sent[begin + q][24:32], 32 * (q - c)), value)
                    lines.append(value)
                halves.append(jnp.concatenate(lines, axis=0))
            block = jnp.concatenate(halves, axis=1)
        feats.append(jnp.concatenate([block, pad], axis=0).T.astype(BF16))
    data = []
    for tile in range(5):
        columns = []
        for c in range(3):
            if tile < 4:
                block = recv[2 * tile : 2 * tile + 2, 160 * c : 160 * c + 128, :]
            else:
                block = recv[:, 160 * c + 128 : 160 * c + 160, :]
            columns.append(block.reshape(256, 128))
        data.append(jnp.concatenate(columns + [feats[tile]], axis=1))
    data = jnp.concatenate(data, axis=0)
    for part in range(4):
        here = slice(256 * part, 256 * part + 256)
        value = jnp.dot(picks(targets, part), data, preferred_element_type=F32).astype(BF16)
        packed[here, :] = value[:, 0:384]
        extras[here, :] = value[:, 384:512]
    for fetch in fetches:
        fetch.wait()


def compact(lengths, recv, weights, rows):
    vmem, hbm = pl.BlockSpec(memory_space=pltpu.VMEM), pl.BlockSpec(memory_space=pltpu.HBM)
    return pl.pallas_call(
        compact_kernel,
        out_shape=(
            jax.ShapeDtypeStruct((1024, 384), BF16),
            jax.ShapeDtypeStruct((1024, 128), BF16),
            jax.ShapeDtypeStruct(weights.shape, BF16),
            jax.ShapeDtypeStruct(rows.shape, BF16),
        ),
        in_specs=[pl.BlockSpec(memory_space=pltpu.SMEM), vmem, hbm, hbm],
        out_specs=(vmem, vmem, vmem, vmem),
        scratch_shapes=[pltpu.SemaphoreType.DMA((2,))],
        compiler_params=pltpu.CompilerParams(vmem_limit_bytes=24 * MIB),
    )(lengths, recv, fixed(weights, pltpu.HBM), fixed(rows, pltpu.HBM))


def normal_kernel(packed, weights, rows, out):
    field = packed[...]
    edges = coded(jnp.dot(rows[...], field, preferred_element_type=F32))
    spare = jnp.zeros((120, edges.shape[1]), F32)
    for part in range(4):
        here = slice(256 * part, 256 * part + 256)
        edge = jnp.concatenate([edges[8 * part : 8 * part + 8], spare], axis=0).astype(BF16)
        block = jnp.concatenate([field[here], edge], axis=0)
        value = jnp.dot(weights[0, here, :], block, preferred_element_type=F32)
        value = value + jnp.dot(weights[1, here, :], block, preferred_element_type=F32)
        for c in range(3):
            block = value[:, 128 * c : 128 * c + 128].astype(BF16).reshape(16, 16, 128)
            for half in range(2):
                at = 8 * COL.index(2 * part + half)
                out[at : at + 8, 16 * c : 16 * c + 16, :] = block[8 * half : 8 * half + 8]


def normal(packed, weights, rows):
    vmem = pl.BlockSpec(memory_space=pltpu.VMEM)
    return pl.pallas_call(
        normal_kernel,
        out_shape=jax.ShapeDtypeStruct((64, 48, 128), BF16),
        in_specs=[vmem, vmem, vmem],
        out_specs=vmem,
        compiler_params=pltpu.CompilerParams(vmem_limit_bytes=24 * MIB),
        cost_estimate=pl.CostEstimate(flops=1_600_000_000, bytes_accessed=6_000_000, transcendentals=0),
    )(packed, weights, rows)


def stream_kernel(packed, partner, extras, weights, sent, out):
    for c in range(3):
        columns = slice(128 * c, 128 * c + 128)
        field = jnp.concatenate([packed[:, columns], partner[:, columns], extras[...]], axis=1)
        matrix = jnp.concatenate(
            [weights[:, 0:256], weights[:, 256 + 128 * c : 384 + 128 * c]], axis=1
        )
        value = lax.dot_general(field, matrix, NT, preferred_element_type=F32)
        value = value[:, 0:128] + value[:, 128:256]
        block = value.astype(BF16).reshape(64, 16, 128)
        for run in range(8):
            at = 8 * COL.index(run)
            out[at : at + 8, 16 * c : 16 * c + 16, :] = block[8 * run : 8 * run + 8]
        out[:, 48 + 16 * c : 64 + 16 * c, :] = sent[:, 16 * c : 16 * c + 16, :]


def stream(packed, partner, extras, weights, sent):
    vmem = pl.BlockSpec(memory_space=pltpu.VMEM)
    return pl.pallas_call(
        stream_kernel,
        out_shape=jax.ShapeDtypeStruct((64, 96, 128), BF16),
        in_specs=[vmem] * 5,
        out_specs=vmem,
        compiler_params=pltpu.CompilerParams(vmem_limit_bytes=24 * MIB),
    )(packed, partner, extras, weights, sent)


def unpack_kernel(recv, out_x, out_y, held, sems):
    copies = []
    for which, out in enumerate((out_x, out_y)):
        for c in range(3):
            at = 48 * which + 16 * c
            for run in range(8):
                begin = 8 * COL.index(run)
                held[which, c, 8 * run : 8 * run + 8] = recv[begin : begin + 8, at : at + 16, :]
            copy = pltpu.make_async_copy(held.at[which, c], out.at[c], sems.at[3 * which + c])
            copy.start()
            copies.append(copy)
    for copy in copies:
        copy.wait()


def unpack(recv):
    shape = jax.ShapeDtypeStruct((3, 64, 16, 128), BF16)
    anywhere = pl.BlockSpec(memory_space=pl.ANY)
    return pl.pallas_call(
        unpack_kernel,
        out_shape=(shape, shape),
        in_specs=[pl.BlockSpec(memory_space=pltpu.VMEM)],
        out_specs=(anywhere, anywhere),
        scratch_shapes=[pltpu.VMEM((2, 3, 64, 16, 128), BF16), pltpu.SemaphoreType.DMA((6,))],
        compiler_params=pltpu.CompilerParams(vmem_limit_bytes=24 * MIB),
    )(recv)


def local(velocity, lengths, inverse_x, inverse_y, metric):
    rank = lax.axis_index("row")
    where = jnp.stack([lax.shift_right_logical(rank, 1), rank & 1]).astype(jnp.int32)
    sent = pack(velocity[:, 0], inverse_x)
    weights = build_weights(where, inverse_x, inverse_y, metric.reshape(8, 128))
    received = lax.all_to_all(
        sent, "row", split_axis=0, concat_axis=0, tiled=True, axis_index_groups=[list(ROW)]
    )
    received, (weights_y, rows, weights_x) = lax.optimization_barrier((received, weights))
    packed, extras, weights_y, rows = compact(lengths, received, weights_y, rows)
    partner = lax.ppermute(packed, "row", [(i, i ^ 1) for i in range(8)])
    result = normal(packed, weights_y, rows)
    result = stream(packed, partner, extras, weights_x, result)
    moved = lax.all_to_all(
        result,
        "col",
        split_axis=0,
        concat_axis=0,
        tiled=True,
        axis_index_groups=[[8 * run + i for run in COL for i in range(8)]],
    )
    return unpack(moved)


def solution(mesh):
    return jax.shard_map(
        local,
        mesh=mesh,
        in_specs=(P(None, "col", "row", None), P("col", None), P(), P(), P()),
        out_specs=(P(None, None, "col", "row"), P(None, None, "col", "row")),
        check_vma=False,
    )
```
